32 devices in a mesh: section: 2 (over core), fsdp: 4 (over y, x), tensor: 4 (over z).
Axes of the slice: x: 2, y: 2, z: 4, core: 2. Of those that a mesh axis runs over, the one named last changes fastest.
Arguments:
- hidden: bfloat16 [2, 512, 8192], P('section', 'fsdp', 'tensor'), may hold values from -16 to 16
- encoder_weight: bfloat16 [2, 1024, 8192], P('section', 'fsdp', 'tensor'), may hold values from -0.0625 to 0.0625
- decoder_weight: bfloat16 [2, 1024, 8192], P('section', 'fsdp', 'tensor'), may hold values from -16 to 16
- query_weight: bfloat16 [2, 8192, 8192], P('section', 'fsdp', 'tensor'), may hold values from -32 to 32
- key_weight: bfloat16 [2, 8192, 1024], P('section', 'fsdp', 'tensor'), may hold values from -1 to 1
- value_weight: bfloat16 [2, 8192, 1024], P('section', 'fsdp', 'tensor'), may hold values from -0.0625 to 0.0625
- segments: int32 [2, 4, 128], P('section', 'fsdp'), may hold values from 0 to 3, never falling along the last dimension, each value on 1 to 64 neighbouring positions
- out_grad: bfloat16 [2, 512, 8192], P('section', 'fsdp', 'tensor'), may hold values from -6 to 6
Outputs:
- attention: bfloat16 [2, 512, 8192], P('section', 'fsdp', 'tensor')
- hidden_grad: bfloat16 [2, 512, 8192], P('section', 'fsdp', 'tensor')
- encoder_grad: float32 [2, 1024, 8192], P('section', 'fsdp', 'tensor')
- decoder_grad: float32 [2, 1024, 8192], P('section', 'fsdp', 'tensor')
The draws below stay inside these ranges and needn't reach their ends.
Inputs may be any that keep to these rules, and one draw needn't show every extreme that they name: `segments`: segment ids never fall along a row, and attention stays inside one document of one row; each document spans at most 64 tokens, and some document spans exactly that many.
All inputs are finite; a program needn't handle non-finite values.
Results may differ from the reference program's by a relative error of at most 0.025.
Values may be sent and summed in bfloat16 or wider, within the bound.
A program may use at most 128 MiB of HBM per device.

```python
import math
import jax
import jax.numpy as jnp
import numpy as np
from jax import lax

D = 8192
KVH = 8
DH = 128
HQ = 64
R = 1024
TOK_DEV = 128
SECTIONS = 2
TOKENS = 512
SEGS = 4
DOC_MOST = 64
N_FSDP = 4
N_TENSOR = 4


def head_pair(key):
    key_part = jax.random.normal(jax.random.fold_in(key, 101), (SECTIONS, D, KVH * DH), jnp.float32) * D ** (-0.5)
    query_part = jax.random.normal(jax.random.fold_in(key, 102), (SECTIONS, D, HQ * DH), jnp.float32) * D ** (-0.5)
    return (jnp.clip(query_part, -32.0, 32.0), jnp.clip(key_part, -1.0, 1.0))


def draw_query_weight(key, part):
    return head_pair(key)[0].astype(jnp.bfloat16)


def draw_key_weight(key, part):
    return head_pair(key)[1].astype(jnp.bfloat16)


def draw_hidden(key, part):
    shape = (SECTIONS, TOKENS, D)
    base = jax.random.normal(jax.random.fold_in(key, 201), shape, jnp.float32)
    row_scale = jnp.exp(jax.random.uniform(jax.random.fold_in(key, 202), (SECTIONS, TOKENS, 1), jnp.float32, math.log(0.3), math.log(3.0)))
    return jnp.clip(base * row_scale, -16.0, 16.0).astype(jnp.bfloat16)


def draw_decoder_weight(key, part):
    rising = jnp.exp(jnp.linspace(math.log(0.6), math.log(1.8), D)).astype(jnp.float32)
    column_scale = jnp.exp(jax.random.uniform(jax.random.fold_in(key, 302), (SECTIONS, 1, D), jnp.float32, math.log(0.5), math.log(2.0)))
    base = jax.random.normal(jax.random.fold_in(key, 301), (SECTIONS, R, D), jnp.float32) * R ** (-0.5)
    return jnp.clip(base * column_scale * rising[None, None, :], -16.0, 16.0).astype(jnp.bfloat16)


def block_scale(key, extent, cuts, low, largest):
    def one(position, parts):
        heights = jax.random.uniform(jax.random.fold_in(jax.random.fold_in(key, 6), position), (parts,), jnp.float32, low / len(cuts), largest / len(cuts))
        return jnp.repeat(jnp.exp(heights), extent[position] // parts).reshape((-1,) + (1,) * (len(extent) - position - 1))

    factor_of = one(*cuts[0])
    for cut in cuts[1:]:
        factor_of = factor_of * one(*cut)
    return factor_of


def length_profile(amount, total, reach, slope):
    loads = [(1 << 20) // math.isqrt(grade ** slope) + 1 for grade in range(2, amount + 1)]
    spare, holding = total - reach - (amount - 1), [1] * (amount - 1)
    while spare > 0:
        free = [i for i in range(amount - 1) if holding[i] < reach]
        pool, budget = sum([loads[i] for i in free]), spare
        for i in free:
            more = min(reach - holding[i], max(1, budget * loads[i] // pool), spare)
            holding[i] = holding[i] + more
            spare = spare - more
    return np.array([reach] + holding)


def uneven(key, amount, total, reach, skew):
    if amount == 2:
        one = jax.random.randint(key, (), max(1, total - reach), min(reach, total - 1) + 1)
        return jnp.stack([one, total - one])
    sizes = jnp.asarray(length_profile(amount, total, reach, skew), jnp.int32)
    couples = (amount - 1) // 2
    source_of, receiver = sizes[1:1 + 2 * couples:2], sizes[2:2 + 2 * couples:2]
    slack = jnp.minimum(source_of - 1, reach - receiver)
    shifted = jax.random.randint(jax.random.fold_in(key, 1), (couples,), 0, 1 << 20) % (slack + 1)
    sizes = sizes.at[1:1 + 2 * couples:2].set(source_of - shifted).at[2:2 + 2 * couples:2].set(receiver + shifted)
    return sizes[jax.random.permutation(jax.random.fold_in(key, 2), amount)]


def scatter_about(stream_key, dims, spread, most, cuts=(), kind=jnp.bfloat16):
    level = block_scale(stream_key, dims, cuts, -0.22, 0.18) if cuts else 1.0
    drawn = jax.random.normal(stream_key, dims, jnp.float32) * spread * level
    return jnp.minimum(jnp.maximum(drawn, -most), most).astype(kind)


def setup_inputs(seed: int = 0) -> dict:
    keys = jax.random.split(jax.random.key(seed), 9)
    return {
        "hidden": draw_hidden(jax.random.fold_in(keys[8], 71), 0),
        "encoder_weight": scatter_about(keys[1], (SECTIONS, R, D), D ** -0.5, 0.0625, ((0, 2), (1, 4), (2, 4))),
        "decoder_weight": draw_decoder_weight(jax.random.fold_in(keys[8], 71), 0),
        "query_weight": draw_query_weight(jax.random.fold_in(keys[8], 71), 0),
        "key_weight": draw_key_weight(jax.random.fold_in(keys[8], 71), 0),
        "value_weight": scatter_about(keys[5], (SECTIONS, D, KVH * DH), D ** -0.5, 0.0625, ((0, 2), (1, 4), (2, 4))),
        "segments": jax.vmap(lambda own: jnp.searchsorted(jnp.cumsum(uneven(own, SEGS, TOK_DEV, DOC_MOST, 2)), jnp.arange(TOK_DEV), side="right"))(jax.random.split(keys[6], SECTIONS * N_FSDP)).reshape((SECTIONS, N_FSDP, TOK_DEV)).astype(jnp.int32),
        "out_grad": scatter_about(keys[7], (SECTIONS, TOKENS, HQ * DH), 1.0, 6.0, ((0, 2), (1, 4), (2, 4))),
    }


NORM_EPS = 1e-05
ROPE_BASE = 500000.0
NEG_FILL = -1e+30

def rope_tables(segment_row, dim):
    length = segment_row.shape[0]
    positions = jnp.arange(length, dtype=jnp.int32)
    earlier = lax.optimization_barrier(jnp.sum((segment_row[None, :] < segment_row[:, None]).astype(jnp.int32), axis=1))
    places = (positions - earlier).astype(jnp.float32)
    frequency = jnp.exp(jnp.arange(0, dim, 2).astype(jnp.float32) * (-math.log(ROPE_BASE) / dim))
    angles = places[:, None] * frequency[None, :]
    allowed = (segment_row[None, :] == segment_row[:, None]) & (positions[None, :] <= positions[:, None])
    return (jnp.cos(angles), jnp.sin(angles), allowed)

def rotate(values, cosine, sine):
    half_dim = values.shape[-1] // 2
    first_half = values[..., :half_dim]
    second_half = values[..., half_dim:]
    cosine_rows = cosine[:, None, :]
    sine_rows = sine[:, None, :]
    return jnp.concatenate([first_half * cosine_rows - second_half * sine_rows, second_half * cosine_rows + first_half * sine_rows], axis=-1)

def unrotate(grads, cosine, sine):
    half_dim = grads.shape[-1] // 2
    first_half = grads[..., :half_dim]
    second_half = grads[..., half_dim:]
    cosine_rows = cosine[:, None, :]
    sine_rows = sine[:, None, :]
    return jnp.concatenate([first_half * cosine_rows + second_half * sine_rows, second_half * cosine_rows - first_half * sine_rows], axis=-1)

def product(form, left, right):
    return jnp.einsum(form, left.astype(jnp.float32), right.astype(jnp.float32))

def attend(queries, keys_in, values_in, upstream, segment_row, head_count, pair_count):
    length = queries.shape[0]
    group_size = head_count // pair_count
    cosine, sine, allowed = rope_tables(segment_row, DH)
    query_rot = rotate(queries.reshape(length, head_count, DH), cosine, sine).astype(jnp.bfloat16).reshape(length, pair_count, group_size, DH)
    key_rot = rotate(keys_in.reshape(length, pair_count, DH), cosine, sine).astype(jnp.bfloat16)
    value_heads = values_in.reshape(length, pair_count, DH).astype(jnp.bfloat16)
    factor = 1.0 / math.sqrt(DH)
    scores = product('tkgd,skd->kgts', query_rot, key_rot) * factor
    scores = jnp.where(allowed, scores, NEG_FILL)
    row_max = lax.optimization_barrier(jnp.max(scores, axis=-1, keepdims=True))
    exponent = jnp.exp(scores - row_max)
    probs = exponent / lax.optimization_barrier(jnp.sum(exponent, axis=-1, keepdims=True))
    probs_low = probs.astype(jnp.bfloat16)
    mixed = product('kgts,skd->tkgd', probs_low, value_heads).reshape(length, head_count * DH)
    cot_heads = upstream.reshape(length, pair_count, group_size, DH)
    prob_grad = product('tkgd,skd->kgts', cot_heads, value_heads)
    value_grad = product('kgts,tkgd->skd', probs_low, cot_heads)
    score_grad = probs * (prob_grad - lax.optimization_barrier(jnp.sum(probs * prob_grad, axis=-1, keepdims=True)))
    score_grad_low = score_grad.astype(jnp.bfloat16)
    query_grad = product('kgts,skd->tkgd', score_grad_low, key_rot) * factor
    key_grad = product('kgts,tkgd->skd', score_grad_low, query_rot) * factor
    query_grad = unrotate(query_grad.reshape(length, head_count, DH), cosine, sine).reshape(length, head_count * DH)
    key_grad = unrotate(key_grad, cosine, sine).reshape(length, pair_count * DH)
    return (mixed.astype(jnp.bfloat16), query_grad.astype(jnp.bfloat16), key_grad.astype(jnp.bfloat16), value_grad.reshape(length, pair_count * DH).astype(jnp.bfloat16))

def rounded(values):
    low = lax.optimization_barrier(values.astype(jnp.bfloat16))
    return low.astype(jnp.float32)

def block_sum(left, right):
    total = jnp.zeros((left.shape[1], right.shape[1]), jnp.float32)
    for block_index in range(N_FSDP):
        lower = block_index * TOK_DEV
        term = jnp.dot(left[lower:lower + TOK_DEV].T, right[lower:lower + TOK_DEV], preferred_element_type=jnp.float32)
        total = total + rounded(term)
    return total

def reference(hidden, encoder_weight, decoder_weight, query_weight, key_weight, value_weight, segments, out_grad):
    codes = []
    for section_index in range(SECTIONS):
        codes.append(jnp.dot(hidden[section_index], encoder_weight[section_index].T, preferred_element_type=jnp.float32).astype(jnp.bfloat16))
    query_cols = HQ * DH // N_TENSOR
    key_cols = KVH * DH // N_TENSOR
    attention_list = []
    decoder_list = []
    code_grad_list = []
    for section_index in range(SECTIONS):
        code_received = codes[(section_index - 1) % SECTIONS]
        decoded = jnp.dot(code_received, decoder_weight[section_index], preferred_element_type=jnp.float32)
        norm_factor = lax.rsqrt(lax.optimization_barrier(jnp.mean(decoded * decoded, axis=1, keepdims=True)) + NORM_EPS)
        normed = (decoded * norm_factor).astype(jnp.bfloat16)
        queries = jnp.dot(normed, query_weight[section_index], preferred_element_type=jnp.float32)
        keys_all = jnp.dot(normed, key_weight[section_index], preferred_element_type=jnp.float32)
        values_all = jnp.dot(normed, value_weight[section_index], preferred_element_type=jnp.float32)
        mixed_rows, query_rows, key_rows, value_rows = ([], [], [], [])
        for block_index in range(N_FSDP):
            lower = block_index * TOK_DEV
            upper = lower + TOK_DEV
            result = attend(queries[lower:upper], keys_all[lower:upper], values_all[lower:upper], out_grad[section_index, lower:upper], segments[section_index, block_index], HQ, KVH)
            mixed_rows.append(result[0])
            query_rows.append(result[1])
            key_rows.append(result[2])
            value_rows.append(result[3])
        attention_list.append(jnp.concatenate(mixed_rows, axis=0))
        query_grad = jnp.concatenate(query_rows, axis=0)
        key_grad = jnp.concatenate(key_rows, axis=0)
        value_grad = jnp.concatenate(value_rows, axis=0)
        normed_grad = jnp.zeros((TOKENS, D), jnp.float32)
        for group_index in range(N_TENSOR):
            q_lo = group_index * query_cols
            k_lo = group_index * key_cols
            partial_value = jnp.dot(query_grad[:, q_lo:q_lo + query_cols], query_weight[section_index][:, q_lo:q_lo + query_cols].T, preferred_element_type=jnp.float32)
            partial_value = partial_value + jnp.dot(key_grad[:, k_lo:k_lo + key_cols], key_weight[section_index][:, k_lo:k_lo + key_cols].T, preferred_element_type=jnp.float32)
            partial_value = partial_value + jnp.dot(value_grad[:, k_lo:k_lo + key_cols], value_weight[section_index][:, k_lo:k_lo + key_cols].T, preferred_element_type=jnp.float32)
            normed_grad = normed_grad + rounded(partial_value)
        inner_dot = lax.optimization_barrier(jnp.sum(normed_grad * decoded, axis=1, keepdims=True))
        decoded_grad = (norm_factor * normed_grad - decoded * norm_factor ** 3 * inner_dot / D).astype(jnp.bfloat16)
        decoder_list.append(block_sum(code_received, decoded_grad))
        code_grad_list.append(jnp.dot(decoded_grad, decoder_weight[section_index].T, preferred_element_type=jnp.float32).astype(jnp.bfloat16))
    hidden_list = []
    encoder_list = []
    for section_index in range(SECTIONS):
        code_grad = code_grad_list[(section_index + 1) % SECTIONS]
        encoder_list.append(block_sum(code_grad, hidden[section_index]))
        hidden_list.append(jnp.dot(code_grad, encoder_weight[section_index], preferred_element_type=jnp.float32).astype(jnp.bfloat16))
    return (jnp.stack(attention_list), jnp.stack(hidden_list), jnp.stack(encoder_list), jnp.stack(decoder_list))
```

```python
import functools
import math

import jax
import jax.numpy as jnp
from jax import lax
from jax.experimental import pallas as pl
from jax.experimental.pallas import tpu as pltpu
from jax.sharding import PartitionSpec as P

D = 8192
DH = 128


NORM_EPS = 1e-05
ROPE_BASE = 500000.0
NEG_FILL = -1e30


def rope_tables(segment_row, dim):
    length = segment_row.shape[0]
    positions = jnp.arange(length, dtype=jnp.int32)
    earlier = jnp.sum((segment_row[None, :] < segment_row[:, None]).astype(jnp.int32), axis=1)
    places = (positions - earlier).astype(jnp.float32)
    frequency = jnp.exp(jnp.arange(0, dim, 2).astype(jnp.float32) * (-math.log(ROPE_BASE) / dim))
    angles = places[:, None] * frequency[None, :]
    allowed = (segment_row[None, :] == segment_row[:, None]) & (
        positions[None, :] <= positions[:, None]
    )
    return (jnp.cos(angles), jnp.sin(angles), allowed)


def rotate(values, cosine, sine):
    half_dim = values.shape[-1] // 2
    first_half = values[..., :half_dim]
    second_half = values[..., half_dim:]
    cosine_rows = cosine[:, None, :]
    sine_rows = sine[:, None, :]
    return jnp.concatenate(
        [
            first_half * cosine_rows - second_half * sine_rows,
            second_half * cosine_rows + first_half * sine_rows,
        ],
        axis=-1,
    )


def unrotate(grads, cosine, sine):
    half_dim = grads.shape[-1] // 2
    first_half = grads[..., :half_dim]
    second_half = grads[..., half_dim:]
    cosine_rows = cosine[:, None, :]
    sine_rows = sine[:, None, :]
    return jnp.concatenate(
        [
            first_half * cosine_rows + second_half * sine_rows,
            second_half * cosine_rows - first_half * sine_rows,
        ],
        axis=-1,
    )


def product(form, left, right):
    return jnp.einsum(form, left, right, preferred_element_type=jnp.float32)


def attend(queries, keys_in, values_in, upstream, segment_row, head_count, pair_count):
    length = queries.shape[0]
    group_size = head_count // pair_count
    cosine, sine, allowed = rope_tables(segment_row, DH)
    query_rot = (
        rotate(queries.reshape(length, head_count, DH), cosine, sine)
        .astype(jnp.bfloat16)
        .reshape(length, pair_count, group_size, DH)
    )
    key_rot = rotate(keys_in.reshape(length, pair_count, DH), cosine, sine).astype(jnp.bfloat16)
    value_heads = values_in.reshape(length, pair_count, DH).astype(jnp.bfloat16)
    factor = 1.0 / math.sqrt(DH)
    scores = product("tkgd,skd->kgts", query_rot, key_rot) * factor
    scores = jnp.where(allowed, scores, NEG_FILL)
    row_max = jnp.max(scores, axis=-1, keepdims=True)
    exponent = jnp.exp(scores - row_max)
    probs = exponent / jnp.sum(exponent, axis=-1, keepdims=True)
    probs_low = probs.astype(jnp.bfloat16)
    mixed = product("kgts,skd->tkgd", probs_low, value_heads).reshape(length, head_count * DH)
    cot_heads = upstream.reshape(length, pair_count, group_size, DH)
    prob_grad = product("tkgd,skd->kgts", cot_heads, value_heads)
    value_grad = product("kgts,tkgd->skd", probs_low, cot_heads)
    score_grad = probs * (prob_grad - jnp.sum(probs * prob_grad, axis=-1, keepdims=True))
    score_grad_low = score_grad.astype(jnp.bfloat16)
    query_grad = product("kgts,skd->tkgd", score_grad_low, key_rot) * factor
    key_grad = product("kgts,tkgd->skd", score_grad_low, query_rot) * factor
    query_grad = unrotate(query_grad.reshape(length, head_count, DH), cosine, sine).reshape(
        length, head_count * DH
    )
    key_grad = unrotate(key_grad, cosine, sine).reshape(length, pair_count * DH)
    return (
        mixed.astype(jnp.bfloat16),
        query_grad.astype(jnp.bfloat16),
        key_grad.astype(jnp.bfloat16),
        value_grad.reshape(length, pair_count * DH).astype(jnp.bfloat16),
    )


MESH = pl.DeviceIdType.MESH


def exchange_kernel(jobs, *refs):
    count = len(jobs)
    ins, outs, sems = refs[:count], refs[count : 2 * count], refs[2 * count :]
    axes = []
    for axis, _ in jobs:
        if axis not in axes:
            axes.append(axis)
    barrier = pltpu.get_barrier_semaphore()
    total = 0
    for axis in axes:
        size = lax.axis_size(axis)
        me = lax.axis_index(axis)
        for k in range(1, size):
            peer = lax.rem(me + k, size)
            pl.semaphore_signal(barrier, inc=1, device_id={axis: peer}, device_id_type=MESH)
        total += size - 1
    pl.semaphore_wait(barrier, total)
    started = []
    for index, (axis, mode) in enumerate(jobs):
        send, recv, own = sems[3 * index : 3 * index + 3]
        size = lax.axis_size(axis)
        me = lax.axis_index(axis)
        for k in range(1, size):
            peer = lax.rem(me + k, size)
            copy = pltpu.make_async_remote_copy(
                src_ref=ins[index] if mode == "gather" else ins[index].at[peer],
                dst_ref=outs[index].at[me],
                send_sem=send.at[k],
                recv_sem=recv.at[k],
                device_id={axis: peer},
                device_id_type=MESH,
            )
            copy.start()
            started.append(copy)
        local = pltpu.make_async_copy(
            ins[index] if mode == "gather" else ins[index].at[me], outs[index].at[me], own
        )
        local.start()
        started.append(local)
    for copy in started:
        copy.wait()


def exchange(number, *work):
    jobs = tuple((axis, mode) for _, axis, mode in work)
    shapes, scratch = [], []
    for value, axis, mode in work:
        size = lax.axis_size(axis)
        shape = (size,) + value.shape if mode == "gather" else value.shape
        shapes.append(jax.ShapeDtypeStruct(shape, value.dtype))
        scratch += [
            pltpu.SemaphoreType.DMA((size,)),
            pltpu.SemaphoreType.DMA((size,)),
            pltpu.SemaphoreType.DMA,
        ]
    return pl.pallas_call(
        functools.partial(exchange_kernel, jobs),
        out_shape=shapes,
        in_specs=[pl.BlockSpec(memory_space=pl.ANY)] * len(work),
        out_specs=[pl.BlockSpec(memory_space=pl.ANY)] * len(work),
        scratch_shapes=scratch,
        compiler_params=pltpu.CompilerParams(collective_id=number, has_side_effects=True),
    )(*[value for value, _, _ in work])


def code_forward_kernel(chunk_ref, out_ref, send, recv):
    sections, rows, cols = lax.axis_size("section"), lax.axis_size("fsdp"), lax.axis_size("tensor")
    s, f, t = lax.axis_index("section"), lax.axis_index("fsdp"), lax.axis_index("tensor")
    fold = cols // rows
    after, before = lax.rem(s + 1, sections), lax.rem(s + sections - 1, sections)
    barrier = pltpu.get_barrier_semaphore()
    for r in range(rows):
        for u in range(fold):
            pl.semaphore_signal(
                barrier, inc=1, device_id=(before, r, f * fold + u), device_id_type=MESH
            )
    pl.semaphore_wait(barrier, cols)
    slot = f * fold + lax.rem(t, fold)
    copies = []
    for k in range(cols):
        copy = pltpu.make_async_remote_copy(
            src_ref=chunk_ref,
            dst_ref=out_ref.at[slot],
            send_sem=send.at[k],
            recv_sem=recv.at[slot],
            device_id=(after, t // fold, k),
            device_id_type=MESH,
        )
        copy.start()
        copies.append(copy)
    for k in range(cols):
        pltpu.make_async_remote_copy(
            src_ref=chunk_ref,
            dst_ref=out_ref.at[k],
            send_sem=send.at[k],
            recv_sem=recv.at[k],
            device_id=(after, t // fold, k),
            device_id_type=MESH,
        ).wait_recv()
    for copy in copies:
        copy.wait_send()


def code_forward(number, chunk):
    cols = lax.axis_size("tensor")
    return pl.pallas_call(
        code_forward_kernel,
        out_shape=jax.ShapeDtypeStruct((cols,) + chunk.shape, chunk.dtype),
        in_specs=[pl.BlockSpec(memory_space=pl.ANY)],
        out_specs=pl.BlockSpec(memory_space=pl.ANY),
        scratch_shapes=[pltpu.SemaphoreType.DMA((cols,)), pltpu.SemaphoreType.DMA((cols,))],
        compiler_params=pltpu.CompilerParams(collective_id=number, has_side_effects=True),
    )(chunk)


def code_back_kernel(chunk_ref, out_ref, send, recv):
    sections, cols = lax.axis_size("section"), lax.axis_size("tensor")
    s, f, t = lax.axis_index("section"), lax.axis_index("fsdp"), lax.axis_index("tensor")
    after, before = lax.rem(s + 1, sections), lax.rem(s + sections - 1, sections)
    barrier = pltpu.get_barrier_semaphore()
    for k in range(cols):
        pl.semaphore_signal(barrier, inc=1, device_id=(after, f, k), device_id_type=MESH)
    pl.semaphore_wait(barrier, cols)
    copies = []
    for k in range(cols):
        copy = pltpu.make_async_remote_copy(
            src_ref=chunk_ref,
            dst_ref=out_ref.at[t],
            send_sem=send.at[k],
            recv_sem=recv.at[t],
            device_id=(before, f, k),
            device_id_type=MESH,
        )
        copy.start()
        copies.append(copy)
    for k in range(cols):
        pltpu.make_async_remote_copy(
            src_ref=chunk_ref,
            dst_ref=out_ref.at[k],
            send_sem=send.at[k],
            recv_sem=recv.at[k],
            device_id=(before, f, k),
            device_id_type=MESH,
        ).wait_recv()
    for copy in copies:
        copy.wait_send()


def code_back(number, chunk):
    cols = lax.axis_size("tensor")
    return pl.pallas_call(
        code_back_kernel,
        out_shape=jax.ShapeDtypeStruct((cols,) + chunk.shape, chunk.dtype),
        in_specs=[pl.BlockSpec(memory_space=pl.ANY)],
        out_specs=pl.BlockSpec(memory_space=pl.ANY),
        scratch_shapes=[pltpu.SemaphoreType.DMA((cols,)), pltpu.SemaphoreType.DMA((cols,))],
        compiler_params=pltpu.CompilerParams(collective_id=number, has_side_effects=True),
    )(chunk)


def dot_last(left, right):
    return lax.dot_general(
        left, right, (((1,), (1,)), ((), ())), preferred_element_type=jnp.float32
    )


def dot_first(left, right):
    return lax.dot_general(
        left, right, (((0,), (0,)), ((), ())), preferred_element_type=jnp.float32
    )


def dot(left, right):
    return jnp.dot(left, right, preferred_element_type=jnp.float32)


def summed(parts):
    return jnp.sum(parts.astype(jnp.float32), axis=0)


def as_rows(row):
    return jnp.broadcast_to(row[None, :], (8, row.shape[0]))


def body(
    hidden,
    encoder_weight,
    decoder_weight,
    query_weight,
    key_weight,
    value_weight,
    segments,
    out_grad,
):
    low = jnp.bfloat16
    rows, cols = lax.axis_size("fsdp"), lax.axis_size("tensor")
    fold = cols // rows
    residual, encoder, decoder = hidden[0], encoder_weight[0], decoder_weight[0]
    wq, wk, wv = query_weight[0], key_weight[0], value_weight[0]
    tokens, width = residual.shape
    code_rows = encoder.shape[0]
    query_width, key_width = wq.shape[1], wk.shape[1]

    (hidden_all,) = exchange(0, (residual, "fsdp", "gather"))
    decoder_rows = lax.all_gather(decoder, "fsdp", axis=0, tiled=True)
    hidden_all = hidden_all.reshape(rows * tokens, width)
    chunk = rows * tokens // cols
    code_partial = dot_last(hidden_all, encoder).astype(low).reshape(cols, chunk, code_rows)
    (code_parts,) = exchange(1, (code_partial, "tensor", "scatter"))
    pieces = code_forward(2, summed(code_parts).astype(low))
    code_received = (
        pieces.reshape(rows, fold, chunk, code_rows)
        .transpose(1, 2, 0, 3)
        .reshape(tokens, rows * code_rows)
    )
    decoded = dot(code_received, decoder_rows)
    square_sum = jnp.sum(decoded * decoded, axis=1)
    decoded_all, square_all, encoder_rows = exchange(
        3,
        (decoded.astype(low), "tensor", "gather"),
        (as_rows(square_sum), "tensor", "gather"),
        (encoder, "fsdp", "gather"),
    )
    encoder_rows = encoder_rows.reshape(rows * code_rows, width)
    norm_factor = lax.rsqrt(jnp.sum(square_all[:, 0], axis=0) / D + NORM_EPS)[:, None]
    (columns,) = exchange(
        4, (decoded_all.reshape(rows, fold, tokens, width), "fsdp", "scatter")
    )
    columns = columns.transpose(0, 2, 1, 3).reshape(rows * tokens, fold * width)
    query_parts, key_parts, value_parts = exchange(
        5,
        (dot(columns, wq).astype(low).reshape(rows, tokens, query_width), "fsdp", "scatter"),
        (dot(columns, wk).astype(low).reshape(rows, tokens, key_width), "fsdp", "scatter"),
        (dot(columns, wv).astype(low).reshape(rows, tokens, key_width), "fsdp", "scatter"),
    )
    mixed, query_grad, key_grad, value_grad = attend(
        summed(query_parts) * norm_factor,
        summed(key_parts) * norm_factor,
        summed(value_parts) * norm_factor,
        out_grad[0],
        segments[0, 0],
        query_width // DH,
        key_width // DH,
    )
    code_split = code_received.reshape(tokens, rows, code_rows).transpose(1, 0, 2)
    query_grads, key_grads, value_grads, code_all = exchange(
        6,
        (query_grad, "fsdp", "gather"),
        (key_grad, "fsdp", "gather"),
        (value_grad, "fsdp", "gather"),
        (code_split, "fsdp", "scatter"),
    )
    whole = rows * tokens
    partial_cols = (
        dot_last(query_grads.reshape(whole, query_width), wq)
        + dot_last(key_grads.reshape(whole, key_width), wk)
        + dot_last(value_grads.reshape(whole, key_width), wv)
    ).astype(low)
    (back,) = exchange(7, (partial_cols.reshape(rows, tokens, fold * width), "fsdp", "scatter"))
    back = back.reshape(rows, tokens, fold, width).transpose(0, 2, 1, 3)
    (grad_parts,) = exchange(8, (back.reshape(cols, tokens, width), "tensor", "scatter"))
    normed_grad = summed(grad_parts)
    (inner_parts,) = exchange(
        9, (as_rows(jnp.sum(normed_grad * decoded, axis=1)), "tensor", "gather")
    )
    inner_dot = jnp.sum(inner_parts[:, 0], axis=0)[:, None]
    decoded_grad = (norm_factor * normed_grad - decoded * norm_factor**3 * inner_dot / D).astype(
        low
    )
    grad_partial = dot_last(decoded_grad, decoder_rows).astype(low)
    code_grad_parts, decoded_grads = exchange(
        10,
        (grad_partial.reshape(cols, tokens // cols, rows * code_rows), "tensor", "scatter"),
        (decoded_grad, "fsdp", "gather"),
    )
    code_grad = code_back(11, summed(code_grad_parts).astype(low))
    code_grad = code_grad.reshape(tokens, rows * code_rows)
    (code_grads,) = exchange(
        12, (code_grad.reshape(tokens, rows, code_rows).transpose(1, 0, 2), "fsdp", "scatter")
    )
    hidden_grad = dot(code_grad, encoder_rows).astype(low)
    decoder_grad = dot_first(
        code_all.reshape(whole, code_rows), decoded_grads.reshape(whole, width)
    )
    encoder_grad = dot_first(code_grads.reshape(whole, code_rows), hidden_all)
    return (mixed[None], hidden_grad[None], encoder_grad[None], decoder_grad[None])


def solution(mesh):
    placed = (
        P("section", "fsdp", "tensor"),
        P("section", "fsdp", "tensor"),
        P("section", "fsdp", "tensor"),
        P("section", "fsdp", "tensor"),
        P("section", "fsdp", "tensor"),
        P("section", "fsdp", "tensor"),
        P("section", "fsdp", None),
        P("section", "fsdp", "tensor"),
    )
    return jax.shard_map(
        body,
        mesh=mesh,
        in_specs=placed,
        out_specs=(
            P("section", "fsdp", "tensor"),
            P("section", "fsdp", "tensor"),
            P("section", "fsdp", "tensor"),
            P("section", "fsdp", "tensor"),
        ),
        check_vma=False,
    )
```

```python
import functools
import math

import jax
import jax.numpy as jnp
from jax import lax
from jax.experimental import pallas as pl
from jax.experimental.pallas import tpu as pltpu
from jax.sharding import PartitionSpec as P

D = 8192
DH = 128


NORM_EPS = 1e-05
ROPE_BASE = 500000.0
NEG_FILL = -1e30


def rope_tables(segment_row, dim):
    length = segment_row.shape[0]
    positions = jnp.arange(length, dtype=jnp.int32)
    earlier = jnp.sum((segment_row[None, :] < segment_row[:, None]).astype(jnp.int32), axis=1)
    places = (positions - earlier).astype(jnp.float32)
    frequency = jnp.exp(jnp.arange(0, dim, 2).astype(jnp.float32) * (-math.log(ROPE_BASE) / dim))
    angles = places[:, None] * frequency[None, :]
    allowed = (segment_row[None, :] == segment_row[:, None]) & (
        positions[None, :] <= positions[:, None]
    )
    return (jnp.cos(angles), jnp.sin(angles), allowed)


MESH = pl.DeviceIdType.MESH


CHUNKS = 4


def greet(axes):
    barrier = pltpu.get_barrier_semaphore()
    total = 0
    for axis in axes:
        size = lax.axis_size(axis)
        me = lax.axis_index(axis)
        for k in range(1, size):
            peer = lax.rem(me + k, size)
            pl.semaphore_signal(barrier, inc=1, device_id={axis: peer}, device_id_type=MESH)
        total += size - 1
    pl.semaphore_wait(barrier, total)


def sent(source, target, send, recv, place):
    return pltpu.make_async_remote_copy(
        src_ref=source,
        dst_ref=target,
        send_sem=send,
        recv_sem=recv,
        device_id=place,
        device_id_type=MESH,
    )


class Square:
    def __init__(self, axis, source, target, send, recv, own):
        self.axis, self.source, self.target = axis, source, target
        self.send, self.recv, self.own = send, recv, own
        self.me = lax.axis_index(axis)
        x, y = lax.rem(self.me, 2), self.me // 2
        self.near = (2 * y + (1 - x), 2 * (1 - y) + x)
        self.half = source.shape[0] // 2
        self.copies, self.arrivals = [], []

    def part(self, h):
        return pl.ds(h * self.half, self.half)

    def start(self):
        for order in range(2):
            for side in range(2):
                h = order if side == 0 else 1 - order
                copy = sent(
                    self.source.at[self.part(h)],
                    self.target.at[self.me, self.part(h)],
                    self.send.at[2 * side + h],
                    self.recv.at[2 * side + h],
                    {self.axis: self.near[side]},
                )
                copy.start()
                self.copies.append(copy)
        self.local = pltpu.make_async_copy(self.source, self.target.at[self.me], self.own)
        self.local.start()

    def arrival(self, slot, h, number):
        return sent(
            self.source.at[self.part(h)],
            self.target.at[slot, self.part(h)],
            self.send.at[number],
            self.recv.at[number],
            {self.axis: self.near[0]},
        )

    def forward(self):
        for side in range(2):
            h = side
            self.arrival(self.near[side], h, 2 * side + h).wait_recv()
            piece = self.target.at[self.near[side], self.part(h)]
            copy = sent(
                piece, piece, self.send.at[4 + h], self.recv.at[4 + h],
                {self.axis: self.near[1 - side]},
            )
            copy.start()
            self.copies.append(copy)

    def finish(self):
        for side in range(2):
            h = 1 - side
            self.arrival(self.near[side], h, 2 * side + h).wait_recv()
        for h in range(2):
            self.arrival(3 - self.me, h, 4 + h).wait_recv()
        for copy in self.copies:
            copy.wait_send()
        self.local.wait()


class Direct:
    def __init__(self, axis, mode, source, target, send, recv, own):
        self.axis, self.mode, self.source, self.target = axis, mode, source, target
        self.send, self.recv, self.own = send, recv, own
        self.copies = []

    def start(self):
        size, me = lax.axis_size(self.axis), lax.axis_index(self.axis)
        whole = self.mode == "gather"
        for k in range(1, size):
            peer = lax.rem(me + k, size)
            copy = sent(
                self.source if whole else self.source.at[peer],
                self.target.at[me],
                self.send.at[k],
                self.recv.at[k],
                {self.axis: peer},
            )
            copy.start()
            self.copies.append(copy)
        local = pltpu.make_async_copy(
            self.source if whole else self.source.at[me], self.target.at[me], self.own
        )
        local.start()
        self.copies.append(local)

    def forward(self):
        pass

    def finish(self):
        for copy in self.copies:
            copy.wait()


def transfer(axis, mode, *refs):
    if mode == "gather" and axis == "fsdp" and lax.axis_size(axis) == 4:
        return Square(axis, *refs)
    return Direct(axis, mode, *refs)


def exchange_kernel(jobs, *refs):
    count = len(jobs)
    ins, outs, sems = refs[:count], refs[count : 2 * count], refs[2 * count :]
    greet(sorted({axis for axis, _ in jobs}))
    moves = [
        transfer(axis, mode, ins[i], outs[i], *sems[3 * i : 3 * i + 3])
        for i, (axis, mode) in enumerate(jobs)
    ]
    for move in moves:
        move.start()
    for move in moves:
        move.forward()
    for move in moves:
        move.finish()


def job_scratch(axis):
    size = max(lax.axis_size(axis), 6)
    return [
        pltpu.SemaphoreType.DMA((size,)),
        pltpu.SemaphoreType.DMA((size,)),
        pltpu.SemaphoreType.DMA,
    ]


def any_call(kernel, number, shapes, scratch, *values):
    return pl.pallas_call(
        kernel,
        out_shape=shapes,
        in_specs=[pl.BlockSpec(memory_space=pl.ANY)] * len(values),
        out_specs=[pl.BlockSpec(memory_space=pl.ANY)] * len(shapes),
        scratch_shapes=scratch,
        compiler_params=pltpu.CompilerParams(collective_id=number, has_side_effects=True),
    )(*values)


def exchange(number, *work):
    jobs = tuple((axis, mode) for _, axis, mode in work)
    shapes, scratch = [], []
    for value, axis, mode in work:
        size = lax.axis_size(axis)
        shape = (size,) + value.shape if mode == "gather" else value.shape
        shapes.append(jax.ShapeDtypeStruct(shape, value.dtype))
        scratch += job_scratch(axis)
    return any_call(
        functools.partial(exchange_kernel, jobs), number, shapes, scratch,
        *[value for value, _, _ in work],
    )


def code_forward_kernel(chunk_ref, extra_ref, out_ref, extra_out, send, recv, *sems):
    sections, rows, cols = lax.axis_size("section"), lax.axis_size("fsdp"), lax.axis_size("tensor")
    s, f, t = lax.axis_index("section"), lax.axis_index("fsdp"), lax.axis_index("tensor")
    fold = cols // rows
    after, before = lax.rem(s + 1, sections), lax.rem(s + sections - 1, sections)
    barrier = pltpu.get_barrier_semaphore()
    for r in range(rows):
        for u in range(fold):
            pl.semaphore_signal(
                barrier, inc=1, device_id=(before, r, f * fold + u), device_id_type=MESH
            )
    for k in range(1, rows):
        pl.semaphore_signal(
            barrier, inc=1, device_id=(s, lax.rem(f + k, rows), t), device_id_type=MESH
        )
    pl.semaphore_wait(barrier, cols + rows - 1)
    slot = f * fold + lax.rem(t, fold)
    copies = []
    for k in range(cols):
        copy = sent(
            chunk_ref, out_ref.at[slot], send.at[k], recv.at[slot], (after, t // fold, k)
        )
        copy.start()
        copies.append(copy)
    move = transfer("fsdp", "gather", extra_ref, extra_out, *sems)
    move.start()
    move.forward()
    for k in range(cols):
        sent(
            chunk_ref, out_ref.at[k], send.at[k], recv.at[k], (after, t // fold, k)
        ).wait_recv()
    for copy in copies:
        copy.wait_send()
    move.finish()


def code_forward(number, chunk, extra):
    rows, cols = lax.axis_size("fsdp"), lax.axis_size("tensor")
    return any_call(
        code_forward_kernel,
        number,
        [
            jax.ShapeDtypeStruct((cols,) + chunk.shape, chunk.dtype),
            jax.ShapeDtypeStruct((rows,) + extra.shape, extra.dtype),
        ],
        [pltpu.SemaphoreType.DMA((cols,)), pltpu.SemaphoreType.DMA((cols,))]
        + job_scratch("fsdp"),
        chunk,
        extra,
    )


def spread_kernel(
    own_ref, sum_ref, columns_ref, gathered_ref, sums_ref,
    right_send, right_recv, left_send, left_recv, cross_send, cross_recv, own_sem, *sems
):
    rows, cols = lax.axis_size("fsdp"), lax.axis_size("tensor")
    f, t = lax.axis_index("fsdp"), lax.axis_index("tensor")
    fold = cols // rows
    size = own_ref.shape[0] // CHUNKS
    greet(("fsdp", "tensor"))
    sums = Direct("tensor", "gather", sum_ref, sums_ref, *sems)
    sums.start()

    def piece(ref, c):
        return ref.at[pl.ds(c * size, size)]

    def hop(d, c, block, way):
        source = piece(own_ref if d == 0 else gathered_ref.at[block], c)
        send, recv = (right_send, right_recv) if way > 0 else (left_send, left_recv)
        return sent(
            source, piece(gathered_ref.at[block], c), send.at[d, c], recv.at[d + 1, c],
            {"tensor": t + way},
        )

    def arrived(d, c, block, way):
        recv = right_recv if way > 0 else left_recv
        return sent(
            piece(own_ref, c), piece(gathered_ref.at[block], c), right_send.at[d, c],
            recv.at[d, c], {"tensor": lax.rem(t + 1, cols)},
        )

    def cross(source, c, block):
        target = piece(columns_ref.at[f, lax.rem(block, fold)], c)
        there = block // fold
        remote = sent(
            source, target, cross_send.at[block, c],
            cross_recv.at[f, lax.rem(block, fold), c], {"fsdp": there},
        )
        local = pltpu.make_async_copy(source, target, own_sem.at[lax.rem(block, fold), c])
        return there, remote, local

    def each(act):
        for d in range(cols):
            for c in range(CHUNKS):
                if d == 0:
                    act(d, c, t, 0)
                    continue

                @pl.when(t - d >= 0)
                def _():
                    act(d, c, t - d, 1)

                @pl.when(t + d < cols)
                def _():
                    act(d, c, t + d, -1)

    def begin(d, c, block, way):
        if d > 0:
            arrived(d, c, block, way).wait_recv()
        if way >= 0 and d < cols - 1:

            @pl.when(t + 1 < cols)
            def _():
                hop(d, c, block, 1).start()

        if way <= 0 and d < cols - 1:

            @pl.when(t > 0)
            def _():
                hop(d, c, block, -1).start()

        source = piece(own_ref if d == 0 else gathered_ref.at[block], c)
        there, remote, local = cross(source, c, block)

        @pl.when(there != f)
        def _():
            remote.start()

        @pl.when(there == f)
        def _():
            local.start()

    def end(d, c, block, way):
        if way >= 0 and d < cols - 1:

            @pl.when(t + 1 < cols)
            def _():
                hop(d, c, block, 1).wait_send()

        if way <= 0 and d < cols - 1:

            @pl.when(t > 0)
            def _():
                hop(d, c, block, -1).wait_send()

        source = piece(own_ref if d == 0 else gathered_ref.at[block], c)
        there, remote, local = cross(source, c, block)

        @pl.when(there != f)
        def _():
            remote.wait_send()

        @pl.when(there == f)
        def _():
            local.wait()

    each(begin)
    for k in range(1, rows):
        peer = lax.rem(f + k, rows)
        for u in range(fold):
            for c in range(CHUNKS):
                sent(
                    piece(own_ref, c), piece(columns_ref.at[peer, u], c), cross_send.at[0, c],
                    cross_recv.at[peer, u, c], {"fsdp": peer},
                ).wait_recv()
    each(end)
    sums.finish()


def spread(number, own, sums):
    rows, cols = lax.axis_size("fsdp"), lax.axis_size("tensor")
    fold = cols // rows
    dma = pltpu.SemaphoreType.DMA
    return any_call(
        spread_kernel,
        number,
        [
            jax.ShapeDtypeStruct((rows, fold) + own.shape, own.dtype),
            jax.ShapeDtypeStruct((cols,) + own.shape, own.dtype),
            jax.ShapeDtypeStruct((cols,) + sums.shape, sums.dtype),
        ],
        [dma((cols, CHUNKS)) for _ in range(5)]
        + [dma((rows, fold, CHUNKS)), dma((fold, CHUNKS))]
        + job_scratch("tensor"),
        own,
        sums,
    )


def back_kernel(
    in_ref, out_ref, middle_ref, cross_send, cross_recv, send, recv, own_sem
):
    rows, cols = lax.axis_size("fsdp"), lax.axis_size("tensor")
    f, t = lax.axis_index("fsdp"), lax.axis_index("tensor")
    fold = cols // rows
    size = in_ref.shape[2] // CHUNKS
    greet(("fsdp", "tensor"))

    def piece(ref, c):
        return ref.at[pl.ds(c * size, size)]

    def cross(k, u, c):
        peer = lax.rem(f + k, rows)
        return sent(
            piece(in_ref.at[peer, u], c), piece(middle_ref.at[f, u], c),
            cross_send.at[k, u, c], cross_recv.at[k, u, c], {"fsdp": peer},
        )

    def onward(k, u, c):
        origin = lax.rem(f + rows - k, rows)
        block = origin * fold + u
        source = piece((in_ref if k == 0 else middle_ref).at[origin, u], c)
        target = piece(out_ref.at[t], c)
        remote = sent(source, target, send.at[k, u, c], recv.at[t, c], {"tensor": block})
        return block, remote, pltpu.make_async_copy(source, target, own_sem.at[c])

    def landed(k, u, c):
        origin = lax.rem(f + rows - k, rows)
        return sent(
            piece(in_ref.at[origin, u], c), piece(middle_ref.at[origin, u], c),
            cross_send.at[k, u, c], cross_recv.at[k, u, c], {"fsdp": lax.rem(f + k, rows)},
        )

    order = [(k, u, c) for c in range(CHUNKS) for k in range(rows) for u in range(fold)]
    for k, u, c in order:
        if k > 0:
            cross(k, u, c).start()
    for k, u, c in order:
        if k > 0:
            landed(k, u, c).wait_recv()
        block, remote, local = onward(k, u, c)

        @pl.when(block != t)
        def _():
            remote.start()

        @pl.when(block == t)
        def _():
            local.start()

    for k in range(1, cols):
        peer = lax.rem(t + k, cols)
        for c in range(CHUNKS):
            sent(
                piece(in_ref.at[0, 0], c), piece(out_ref.at[peer], c), send.at[0, 0, c],
                recv.at[peer, c], {"tensor": peer},
            ).wait_recv()
    for k, u, c in order:
        if k > 0:
            cross(k, u, c).wait_send()
        block, remote, local = onward(k, u, c)

        @pl.when(block != t)
        def _():
            remote.wait_send()

        @pl.when(block == t)
        def _():
            local.wait()


def back_to_features(number, parts):
    rows, cols = lax.axis_size("fsdp"), lax.axis_size("tensor")
    fold = cols // rows
    dma = pltpu.SemaphoreType.DMA
    return any_call(
        back_kernel,
        number,
        [
            jax.ShapeDtypeStruct((cols,) + parts.shape[2:], parts.dtype),
            jax.ShapeDtypeStruct(parts.shape, parts.dtype),
        ],
        [dma((rows, fold, CHUNKS)) for _ in range(3)]
        + [dma((cols, CHUNKS)), dma((CHUNKS,))],
        parts,
    )[0]


def attend_kernel(
    group_size, query_ref, key_ref, value_ref, up_ref, cos_ref, sin_ref, norm_ref, allowed_ref,
    mixed_ref, query_grad_ref, key_grad_ref, value_grad_ref
):
    low = jnp.bfloat16
    factor = 1.0 / math.sqrt(DH)
    cosine, sine, norm = cos_ref[...], sin_ref[...], norm_ref[...]
    allowed = allowed_ref[...] > 0

    def total(ref, columns):
        parts = ref[0, :, columns].astype(jnp.float32)
        for r in range(1, ref.shape[0]):
            parts += ref[r, :, columns].astype(jnp.float32)
        return parts * norm

    def turned(values):
        return values * cosine + pltpu.roll(values, DH // 2, 1) * sine

    def turned_back(values):
        return values * cosine - pltpu.roll(values, DH // 2, 1) * sine

    key_rot = turned(total(key_ref, pl.ds(0, DH))).astype(low)
    value = total(value_ref, pl.ds(0, DH)).astype(low)
    key_grad = jnp.zeros(key_rot.shape, jnp.float32)
    value_grad = jnp.zeros(key_rot.shape, jnp.float32)
    for h in range(group_size):
        columns = pl.ds(h * DH, DH)
        query_rot = turned(total(query_ref, columns)).astype(low)
        scores = jnp.where(allowed, dot_last(query_rot, key_rot) * factor, NEG_FILL)
        exponent = jnp.exp(scores - jnp.max(scores, axis=-1, keepdims=True))
        probs = exponent / jnp.sum(exponent, axis=-1, keepdims=True)
        probs_low = probs.astype(low)
        upstream = up_ref[:, columns]
        mixed_ref[:, columns] = dot(probs_low, value).astype(low)
        prob_grad = dot_last(upstream, value)
        value_grad += dot_first(probs_low, upstream)
        score_grad = probs * (prob_grad - jnp.sum(probs * prob_grad, axis=-1, keepdims=True))
        score_low = score_grad.astype(low)
        query_grad_ref[:, columns] = turned_back(dot(score_low, key_rot) * factor).astype(low)
        key_grad += dot_first(score_low, query_rot) * factor
    key_grad_ref[...] = turned_back(key_grad).astype(low)
    value_grad_ref[...] = value_grad.astype(low)


def attend(query_parts, key_parts, value_parts, norm_factor, upstream, segment_row):
    rows, tokens, query_width = query_parts.shape
    pair_count = key_parts.shape[2] // DH
    wide = query_width // pair_count
    cosine, sine, allowed = rope_tables(segment_row, DH)
    fixed = pl.BlockSpec((tokens, DH), lambda g: (0, 0))
    parts = pl.BlockSpec((rows, tokens, DH), lambda g: (0, 0, g))
    one = pl.BlockSpec((tokens, DH), lambda g: (0, g))
    group = pl.BlockSpec((tokens, wide), lambda g: (0, g))
    low = jnp.bfloat16
    return pl.pallas_call(
        functools.partial(attend_kernel, wide // DH),
        grid=(pair_count,),
        out_shape=[
            jax.ShapeDtypeStruct((tokens, query_width), low),
            jax.ShapeDtypeStruct((tokens, query_width), low),
            jax.ShapeDtypeStruct((tokens, pair_count * DH), low),
            jax.ShapeDtypeStruct((tokens, pair_count * DH), low),
        ],
        in_specs=[
            pl.BlockSpec((rows, tokens, wide), lambda g: (0, 0, g)),
            parts, parts, group, fixed, fixed, fixed,
            pl.BlockSpec((tokens, tokens), lambda g: (0, 0)),
        ],
        out_specs=[group, group, one, one],
        compiler_params=pltpu.CompilerParams(vmem_limit_bytes=32 * 1024 * 1024),
    )(
        query_parts, key_parts, value_parts, upstream,
        jnp.concatenate([cosine, cosine], axis=1), jnp.concatenate([-sine, sine], axis=1),
        jnp.broadcast_to(norm_factor, (tokens, DH)), allowed.astype(jnp.float32),
    )


def code_back_kernel(chunk_ref, out_ref, send, recv):
    sections, cols = lax.axis_size("section"), lax.axis_size("tensor")
    s, f, t = lax.axis_index("section"), lax.axis_index("fsdp"), lax.axis_index("tensor")
    after, before = lax.rem(s + 1, sections), lax.rem(s + sections - 1, sections)
    barrier = pltpu.get_barrier_semaphore()
    for k in range(cols):
        pl.semaphore_signal(barrier, inc=1, device_id=(after, f, k), device_id_type=MESH)
    pl.semaphore_wait(barrier, cols)
    copies = []
    for k in range(cols):
        copy = pltpu.make_async_remote_copy(
            src_ref=chunk_ref,
            dst_ref=out_ref.at[t],
            send_sem=send.at[k],
            recv_sem=recv.at[t],
            device_id=(before, f, k),
            device_id_type=MESH,
        )
        copy.start()
        copies.append(copy)
    for k in range(cols):
        pltpu.make_async_remote_copy(
            src_ref=chunk_ref,
            dst_ref=out_ref.at[k],
            send_sem=send.at[k],
            recv_sem=recv.at[k],
            device_id=(before, f, k),
            device_id_type=MESH,
        ).wait_recv()
    for copy in copies:
        copy.wait_send()


def code_back(number, chunk):
    cols = lax.axis_size("tensor")
    return pl.pallas_call(
        code_back_kernel,
        out_shape=jax.ShapeDtypeStruct((cols,) + chunk.shape, chunk.dtype),
        in_specs=[pl.BlockSpec(memory_space=pl.ANY)],
        out_specs=pl.BlockSpec(memory_space=pl.ANY),
        scratch_shapes=[pltpu.SemaphoreType.DMA((cols,)), pltpu.SemaphoreType.DMA((cols,))],
        compiler_params=pltpu.CompilerParams(collective_id=number, has_side_effects=True),
    )(chunk)


def dot_last(left, right):
    return lax.dot_general(
        left, right, (((1,), (1,)), ((), ())), preferred_element_type=jnp.float32
    )


def dot_first(left, right):
    return lax.dot_general(
        left, right, (((0,), (0,)), ((), ())), preferred_element_type=jnp.float32
    )


def dot(left, right):
    return jnp.dot(left, right, preferred_element_type=jnp.float32)


def summed(parts):
    return jnp.sum(parts.astype(jnp.float32), axis=0)


def as_rows(row):
    return jnp.broadcast_to(row[None, :], (8, row.shape[0]))


def body(
    hidden,
    encoder_weight,
    decoder_weight,
    query_weight,
    key_weight,
    value_weight,
    segments,
    out_grad,
):
    low = jnp.bfloat16
    rows, cols = lax.axis_size("fsdp"), lax.axis_size("tensor")
    fold = cols // rows
    residual, encoder, decoder = hidden[0], encoder_weight[0], decoder_weight[0]
    wq, wk, wv = query_weight[0], key_weight[0], value_weight[0]
    tokens, width = residual.shape
    code_rows = encoder.shape[0]
    query_width, key_width = wq.shape[1], wk.shape[1]

    (hidden_all,) = exchange(0, (residual, "fsdp", "gather"))
    hidden_all = hidden_all.reshape(rows * tokens, width)
    chunk = rows * tokens // cols
    code_partial = dot_last(hidden_all, encoder).astype(low).reshape(cols, chunk, code_rows)
    split = code_rows // 2
    code_parts, decoder_upper = exchange(
        1, (code_partial, "tensor", "scatter"), (decoder[:split], "fsdp", "gather")
    )
    pieces, decoder_lower = code_forward(2, summed(code_parts).astype(low), decoder[split:])
    decoder_rows = jnp.concatenate([decoder_upper, decoder_lower], axis=1).reshape(-1, width)
    code_received = (
        pieces.reshape(rows, fold, chunk, code_rows)
        .transpose(1, 2, 0, 3)
        .reshape(tokens, rows * code_rows)
    )
    decoded = dot(code_received, decoder_rows)
    square_sum = jnp.sum(decoded * decoded, axis=1)
    columns, _, square_all = spread(3, decoded.astype(low), as_rows(square_sum))
    norm_factor = lax.rsqrt(jnp.sum(square_all[:, 0], axis=0) / D + NORM_EPS)[:, None]
    columns = columns.transpose(0, 2, 1, 3).reshape(rows * tokens, fold * width)
    query_parts, key_parts, value_parts = exchange(
        5,
        (dot(columns, wq).astype(low).reshape(rows, tokens, query_width), "fsdp", "scatter"),
        (dot(columns, wk).astype(low).reshape(rows, tokens, key_width), "fsdp", "scatter"),
        (dot(columns, wv).astype(low).reshape(rows, tokens, key_width), "fsdp", "scatter"),
    )
    query_parts, encoder = lax.optimization_barrier((query_parts, encoder))
    encoder_rows = lax.all_gather(encoder, "fsdp", axis=0, tiled=True)
    mixed, query_grad, key_grad, value_grad = attend(
        query_parts, key_parts, value_parts, norm_factor, out_grad[0], segments[0, 0]
    )
    code_split = code_received.reshape(tokens, rows, code_rows).transpose(1, 0, 2)
    query_grads, key_grads, value_grads, code_all = exchange(
        6,
        (query_grad, "fsdp", "gather"),
        (key_grad, "fsdp", "gather"),
        (value_grad, "fsdp", "gather"),
        (code_split, "fsdp", "scatter"),
    )
    whole = rows * tokens
    partial_cols = (
        dot_last(query_grads.reshape(whole, query_width), wq)
        + dot_last(key_grads.reshape(whole, key_width), wk)
        + dot_last(value_grads.reshape(whole, key_width), wv)
    ).astype(low)
    partial_cols = partial_cols.reshape(rows, tokens, fold, width).transpose(0, 2, 1, 3)
    grad_parts = back_to_features(7, partial_cols)
    normed_grad = summed(grad_parts)
    (inner_parts,) = exchange(
        9, (as_rows(jnp.sum(normed_grad * decoded, axis=1)), "tensor", "gather")
    )
    inner_dot = jnp.sum(inner_parts[:, 0], axis=0)[:, None]
    decoded_grad = (norm_factor * normed_grad - decoded * norm_factor**3 * inner_dot / D).astype(
        low
    )
    grad_partial = dot_last(decoded_grad, decoder_rows).astype(low)
    code_grad_parts, decoded_grads = exchange(
        10,
        (grad_partial.reshape(cols, tokens // cols, rows * code_rows), "tensor", "scatter"),
        (decoded_grad, "fsdp", "gather"),
    )
    code_grad = code_back(11, summed(code_grad_parts).astype(low))
    code_grad = code_grad.reshape(tokens, rows * code_rows)
    (code_grads,) = exchange(
        12, (code_grad.reshape(tokens, rows, code_rows).transpose(1, 0, 2), "fsdp", "scatter")
    )
    hidden_grad = dot(code_grad, encoder_rows).astype(low)
    decoder_grad = dot_first(
        code_all.reshape(whole, code_rows), decoded_grads.reshape(whole, width)
    )
    encoder_grad = dot_first(code_grads.reshape(whole, code_rows), hidden_all)
    return (mixed[None], hidden_grad[None], encoder_grad[None], decoder_grad[None])


def solution(mesh):
    placed = (
        P("section", "fsdp", "tensor"),
        P("section", "fsdp", "tensor"),
        P("section", "fsdp", "tensor"),
        P("section", "fsdp", "tensor"),
        P("section", "fsdp", "tensor"),
        P("section", "fsdp", "tensor"),
        P("section", "fsdp", None),
        P("section", "fsdp", "tensor"),
    )
    return jax.shard_map(
        body,
        mesh=mesh,
        in_specs=placed,
        out_specs=(
            P("section", "fsdp", "tensor"),
            P("section", "fsdp", "tensor"),
            P("section", "fsdp", "tensor"),
            P("section", "fsdp", "tensor"),
        ),
        check_vma=False,
    )
```

```python
import functools
import math

import jax
import jax.numpy as jnp
from jax import lax
from jax.experimental import pallas as pl
from jax.experimental.pallas import tpu as pltpu
from jax.sharding import PartitionSpec as P

D = 8192
DH = 128


NORM_EPS = 1e-05
ROPE_BASE = 500000.0
NEG_FILL = -1e30


def rope_tables(segment_row, dim):
    length = segment_row.shape[0]
    positions = jnp.arange(length, dtype=jnp.int32)
    earlier = jnp.sum((segment_row[None, :] < segment_row[:, None]).astype(jnp.int32), axis=1)
    places = (positions - earlier).astype(jnp.float32)
    frequency = jnp.exp(jnp.arange(0, dim, 2).astype(jnp.float32) * (-math.log(ROPE_BASE) / dim))
    angles = places[:, None] * frequency[None, :]
    allowed = (segment_row[None, :] == segment_row[:, None]) & (
        positions[None, :] <= positions[:, None]
    )
    return (jnp.cos(angles), jnp.sin(angles), allowed)


MESH = pl.DeviceIdType.MESH


CHUNKS = 4


def greet(axes):
    barrier = pltpu.get_barrier_semaphore()
    total = 0
    for axis in axes:
        size = lax.axis_size(axis)
        me = lax.axis_index(axis)
        for k in range(1, size):
            peer = lax.rem(me + k, size)
            pl.semaphore_signal(barrier, inc=1, device_id={axis: peer}, device_id_type=MESH)
        total += size - 1
    pl.semaphore_wait(barrier, total)


def sent(source, target, send, recv, place):
    return pltpu.make_async_remote_copy(
        src_ref=source,
        dst_ref=target,
        send_sem=send,
        recv_sem=recv,
        device_id=place,
        device_id_type=MESH,
    )


class Square:
    def __init__(self, axis, source, target, send, recv, own):
        self.axis, self.source, self.target = axis, source, target
        self.send, self.recv, self.own = send, recv, own
        self.me = lax.axis_index(axis)
        x, y = lax.rem(self.me, 2), self.me // 2
        self.near = (2 * y + (1 - x), 2 * (1 - y) + x)
        self.half = source.shape[0] // 2
        self.copies, self.arrivals = [], []

    def part(self, h):
        return pl.ds(h * self.half, self.half)

    def start(self):
        for order in range(2):
            for side in range(2):
                h = order if side == 0 else 1 - order
                copy = sent(
                    self.source.at[self.part(h)],
                    self.target.at[self.me, self.part(h)],
                    self.send.at[2 * side + h],
                    self.recv.at[2 * side + h],
                    {self.axis: self.near[side]},
                )
                copy.start()
                self.copies.append(copy)
        self.local = pltpu.make_async_copy(self.source, self.target.at[self.me], self.own)
        self.local.start()

    def arrival(self, slot, h, number):
        return sent(
            self.source.at[self.part(h)],
            self.target.at[slot, self.part(h)],
            self.send.at[number],
            self.recv.at[number],
            {self.axis: self.near[0]},
        )

    def forward(self):
        for side in range(2):
            h = side
            self.arrival(self.near[side], h, 2 * side + h).wait_recv()
            piece = self.target.at[self.near[side], self.part(h)]
            copy = sent(
                piece, piece, self.send.at[4 + h], self.recv.at[4 + h],
                {self.axis: self.near[1 - side]},
            )
            copy.start()
            self.copies.append(copy)

    def finish(self):
        for side in range(2):
            h = 1 - side
            self.arrival(self.near[side], h, 2 * side + h).wait_recv()
        for h in range(2):
            self.arrival(3 - self.me, h, 4 + h).wait_recv()
        for copy in self.copies:
            copy.wait_send()
        self.local.wait()


class Direct:
    def __init__(self, axis, mode, source, target, send, recv, own):
        self.axis, self.mode, self.source, self.target = axis, mode, source, target
        self.send, self.recv, self.own = send, recv, own
        self.copies = []

    def start(self):
        size, me = lax.axis_size(self.axis), lax.axis_index(self.axis)
        whole = self.mode == "gather"
        for k in range(1, size):
            peer = lax.rem(me + k, size)
            copy = sent(
                self.source if whole else self.source.at[peer],
                self.target.at[me],
                self.send.at[k],
                self.recv.at[k],
                {self.axis: peer},
            )
            copy.start()
            self.copies.append(copy)
        local = pltpu.make_async_copy(
            self.source if whole else self.source.at[me], self.target.at[me], self.own
        )
        local.start()
        self.copies.append(local)

    def forward(self):
        pass

    def finish(self):
        for copy in self.copies:
            copy.wait()


def transfer(axis, mode, *refs):
    if mode == "gather" and axis == "fsdp" and lax.axis_size(axis) == 4:
        return Square(axis, *refs)
    return Direct(axis, mode, *refs)


def exchange_kernel(jobs, *refs):
    count = len(jobs)
    ins, outs, sems = refs[:count], refs[count : 2 * count], refs[2 * count :]
    greet(sorted({axis for axis, _ in jobs}))
    moves = [
        transfer(axis, mode, ins[i], outs[i], *sems[3 * i : 3 * i + 3])
        for i, (axis, mode) in enumerate(jobs)
    ]
    for move in moves:
        move.start()
    for move in moves:
        move.forward()
    for move in moves:
        move.finish()


def job_scratch(axis):
    size = max(lax.axis_size(axis), 6)
    return [
        pltpu.SemaphoreType.DMA((size,)),
        pltpu.SemaphoreType.DMA((size,)),
        pltpu.SemaphoreType.DMA,
    ]


def any_call(kernel, number, shapes, scratch, *values):
    return pl.pallas_call(
        kernel,
        out_shape=shapes,
        in_specs=[pl.BlockSpec(memory_space=pl.ANY)] * len(values),
        out_specs=[pl.BlockSpec(memory_space=pl.ANY)] * len(shapes),
        scratch_shapes=scratch,
        compiler_params=pltpu.CompilerParams(collective_id=number, has_side_effects=True),
    )(*values)


def exchange(number, *work):
    jobs = tuple((axis, mode) for _, axis, mode in work)
    shapes, scratch = [], []
    for value, axis, mode in work:
        size = lax.axis_size(axis)
        shape = (size,) + value.shape if mode == "gather" else value.shape
        shapes.append(jax.ShapeDtypeStruct(shape, value.dtype))
        scratch += job_scratch(axis)
    return any_call(
        functools.partial(exchange_kernel, jobs), number, shapes, scratch,
        *[value for value, _, _ in work],
    )


def code_forward_kernel(chunk_ref, extra_ref, out_ref, extra_out, send, recv, *sems):
    sections, rows, cols = lax.axis_size("section"), lax.axis_size("fsdp"), lax.axis_size("tensor")
    s, f, t = lax.axis_index("section"), lax.axis_index("fsdp"), lax.axis_index("tensor")
    fold = cols // rows
    after, before = lax.rem(s + 1, sections), lax.rem(s + sections - 1, sections)
    barrier = pltpu.get_barrier_semaphore()
    for r in range(rows):
        for u in range(fold):
            pl.semaphore_signal(
                barrier, inc=1, device_id=(before, r, f * fold + u), device_id_type=MESH
            )
    for k in range(1, rows):
        pl.semaphore_signal(
            barrier, inc=1, device_id=(s, lax.rem(f + k, rows), t), device_id_type=MESH
        )
    pl.semaphore_wait(barrier, cols + rows - 1)
    slot = f * fold + lax.rem(t, fold)
    copies = []
    for k in range(cols):
        copy = sent(
            chunk_ref, out_ref.at[slot], send.at[k], recv.at[slot], (after, t // fold, k)
        )
        copy.start()
        copies.append(copy)
    move = transfer("fsdp", "gather", extra_ref, extra_out, *sems)
    move.start()
    move.forward()
    for k in range(cols):
        sent(
            chunk_ref, out_ref.at[k], send.at[k], recv.at[k], (after, t // fold, k)
        ).wait_recv()
    for copy in copies:
        copy.wait_send()
    move.finish()


def code_forward(number, chunk, extra):
    rows, cols = lax.axis_size("fsdp"), lax.axis_size("tensor")
    return any_call(
        code_forward_kernel,
        number,
        [
            jax.ShapeDtypeStruct((cols,) + chunk.shape, chunk.dtype),
            jax.ShapeDtypeStruct((rows,) + extra.shape, extra.dtype),
        ],
        [pltpu.SemaphoreType.DMA((cols,)), pltpu.SemaphoreType.DMA((cols,))]
        + job_scratch("fsdp"),
        chunk,
        extra,
    )


def spread_kernel(
    own_ref, sum_ref, columns_ref, gathered_ref, sums_ref,
    right_send, right_recv, left_send, left_recv, cross_send, cross_recv, own_sem, *sems
):
    rows, cols = lax.axis_size("fsdp"), lax.axis_size("tensor")
    f, t = lax.axis_index("fsdp"), lax.axis_index("tensor")
    fold = cols // rows
    size = own_ref.shape[0] // CHUNKS
    greet(("fsdp", "tensor"))
    sums = Direct("tensor", "gather", sum_ref, sums_ref, *sems)
    sums.start()

    def piece(ref, c):
        return ref.at[pl.ds(c * size, size)]

    def hop(d, c, block, way):
        source = piece(own_ref if d == 0 else gathered_ref.at[block], c)
        send, recv = (right_send, right_recv) if way > 0 else (left_send, left_recv)
        return sent(
            source, piece(gathered_ref.at[block], c), send.at[d, c], recv.at[d + 1, c],
            {"tensor": t + way},
        )

    def arrived(d, c, block, way):
        recv = right_recv if way > 0 else left_recv
        return sent(
            piece(own_ref, c), piece(gathered_ref.at[block], c), right_send.at[d, c],
            recv.at[d, c], {"tensor": lax.rem(t + 1, cols)},
        )

    def cross(source, c, block):
        target = piece(columns_ref.at[f, lax.rem(block, fold)], c)
        there = block // fold
        remote = sent(
            source, target, cross_send.at[block, c],
            cross_recv.at[f, lax.rem(block, fold), c], {"fsdp": there},
        )
        local = pltpu.make_async_copy(source, target, own_sem.at[lax.rem(block, fold), c])
        return there, remote, local

    def each(act):
        for d in range(cols):
            for c in range(CHUNKS):
                if d == 0:
                    act(d, c, t, 0)
                    continue

                @pl.when(t - d >= 0)
                def _():
                    act(d, c, t - d, 1)

                @pl.when(t + d < cols)
                def _():
                    act(d, c, t + d, -1)

    def begin(d, c, block, way):
        if d > 0:
            arrived(d, c, block, way).wait_recv()
        if way >= 0 and d < cols - 1:

            @pl.when(t + 1 < cols)
            def _():
                hop(d, c, block, 1).start()

        if way <= 0 and d < cols - 1:

            @pl.when(t > 0)
            def _():
                hop(d, c, block, -1).start()

        source = piece(own_ref if d == 0 else gathered_ref.at[block], c)
        there, remote, local = cross(source, c, block)

        @pl.when(there != f)
        def _():
            remote.start()

        @pl.when(there == f)
        def _():
            local.start()

    def end(d, c, block, way):
        if way >= 0 and d < cols - 1:

            @pl.when(t + 1 < cols)
            def _():
                hop(d, c, block, 1).wait_send()

        if way <= 0 and d < cols - 1:

            @pl.when(t > 0)
            def _():
                hop(d, c, block, -1).wait_send()

        source = piece(own_ref if d == 0 else gathered_ref.at[block], c)
        there, remote, local = cross(source, c, block)

        @pl.when(there != f)
        def _():
            remote.wait_send()

        @pl.when(there == f)
        def _():
            local.wait()

    each(begin)
    for k in range(1, rows):
        peer = lax.rem(f + k, rows)
        for u in range(fold):
            for c in range(CHUNKS):
                sent(
                    piece(own_ref, c), piece(columns_ref.at[peer, u], c), cross_send.at[0, c],
                    cross_recv.at[peer, u, c], {"fsdp": peer},
                ).wait_recv()
    each(end)
    sums.finish()


def spread(number, own, sums):
    rows, cols = lax.axis_size("fsdp"), lax.axis_size("tensor")
    fold = cols // rows
    dma = pltpu.SemaphoreType.DMA
    return any_call(
        spread_kernel,
        number,
        [
            jax.ShapeDtypeStruct((rows, fold) + own.shape, own.dtype),
            jax.ShapeDtypeStruct((cols,) + own.shape, own.dtype),
            jax.ShapeDtypeStruct((cols,) + sums.shape, sums.dtype),
        ],
        [dma((cols, CHUNKS)) for _ in range(5)]
        + [dma((rows, fold, CHUNKS)), dma((fold, CHUNKS))]
        + job_scratch("tensor"),
        own,
        sums,
    )


def back_kernel(
    *refs
):
    grads, weights, code_ref, (out_ref, code_out) = refs[:3], refs[3:6], refs[6], refs[7:9]
    held, loaded, (product_ref, middle_ref) = refs[9:12], refs[12:15], refs[15:17]
    gather_send, gather_recv, load_sem = refs[17:20]
    cross_send, cross_recv, send, recv, own_sem = refs[20:25]
    code_sems = refs[25:]
    rows, cols = lax.axis_size("fsdp"), lax.axis_size("tensor")
    f, t = lax.axis_index("fsdp"), lax.axis_index("tensor")
    fold = cols // rows
    width = product_ref.shape[3]
    size = product_ref.shape[2] // CHUNKS
    order = [0, 2, 1, 3] if rows == 4 else list(range(rows))
    loads = [
        pltpu.make_async_copy(weights[i], loaded[i], load_sem.at[i]) for i in range(3)
    ]
    owns = [
        pltpu.make_async_copy(grads[i], held[i].at[0], load_sem.at[3 + i]) for i in range(3)
    ]
    for copy in loads + owns:
        copy.start()
    greet(("fsdp", "tensor"))

    def away(k):
        return lax.rem(f + k, rows)

    def origin(k):
        return lax.rem(f + rows - k, rows)

    def spread_out(k, i):
        return sent(
            grads[i], held[i].at[k], gather_send.at[i, k], gather_recv.at[i, k],
            {"fsdp": away(k)},
        )

    for k in order[1:]:
        for i in range(3):
            spread_out(k, i).start()
    codes = Direct("fsdp", "scatter", code_ref, code_out, *code_sems)
    codes.start()

    def piece(ref, c):
        return ref.at[pl.ds(c * size, size)]

    def cross(k, u, c):
        return sent(
            piece(product_ref.at[k, u], c), piece(middle_ref.at[k, u], c),
            cross_send.at[k, u, c], cross_recv.at[k, u, c], {"fsdp": origin(k)},
        )

    def onward(k, u, c):
        block = away(k) * fold + u
        source = piece((product_ref if k == 0 else middle_ref).at[k, u], c)
        target = piece(out_ref.at[t], c)
        remote = sent(source, target, send.at[k, u, c], recv.at[t, c], {"tensor": block})
        return block, remote, pltpu.make_async_copy(source, target, own_sem.at[c])

    def pass_on(k, u, c):
        block, remote, local = onward(k, u, c)

        @pl.when(block != t)
        def _():
            remote.start()

        @pl.when(block == t)
        def _():
            local.start()

    for copy in loads + owns:
        copy.wait()
    tile = min(width, 512)
    for k in order:
        if k > 0:
            for i in range(3):
                spread_out(k, i).wait_recv()
        for u in range(fold):

            @pl.loop(0, width // tile)
            def _(n):
                lower = pl.multiple_of(u * width + n * tile, tile)
                total = dot_last(held[0][k], loaded[0][pl.ds(lower, tile), :])
                for i in range(1, 3):
                    total += dot_last(held[i][k], loaded[i][pl.ds(lower, tile), :])
                columns = pl.ds(pl.multiple_of(n * tile, tile), tile)
                product_ref[k, u, :, columns] = total.astype(product_ref.dtype)

            for c in range(CHUNKS):
                if k == 0:
                    pass_on(k, u, c)
                else:
                    cross(k, u, c).start()
    for k in order[1:]:
        for u in range(fold):
            for c in range(CHUNKS):
                cross(k, u, c).wait_recv()
                pass_on(k, u, c)
    for k in range(1, cols):
        peer = lax.rem(t + k, cols)
        for c in range(CHUNKS):
            sent(
                piece(middle_ref.at[0, 0], c), piece(out_ref.at[peer], c), send.at[0, 0, c],
                recv.at[peer, c], {"tensor": peer},
            ).wait_recv()
    for k in order:
        for i in range(3):
            if k > 0:
                spread_out(k, i).wait_send()
        for u in range(fold):
            for c in range(CHUNKS):
                if k > 0:
                    cross(k, u, c).wait_send()
                block, remote, local = onward(k, u, c)

                @pl.when(block != t)
                def _():
                    remote.wait_send()

                @pl.when(block == t)
                def _():
                    local.wait()

    codes.finish()


def back_to_features(number, grads, weights, codes):
    rows, cols = lax.axis_size("fsdp"), lax.axis_size("tensor")
    fold = cols // rows
    dma = pltpu.SemaphoreType.DMA
    tokens, low = grads[0].shape[0], jnp.bfloat16
    width = weights[0].shape[0] // fold
    return pl.pallas_call(
        back_kernel,
        out_shape=[
            jax.ShapeDtypeStruct((cols, tokens, width), low),
            jax.ShapeDtypeStruct(codes.shape, codes.dtype),
        ],
        in_specs=[pl.BlockSpec(memory_space=pl.ANY)] * 7,
        out_specs=[pl.BlockSpec(memory_space=pl.ANY)] * 2,
        scratch_shapes=[pltpu.VMEM((rows,) + grad.shape, low) for grad in grads]
        + [pltpu.VMEM(weight.shape, low) for weight in weights]
        + [pltpu.VMEM((rows, fold, tokens, width), low)] * 2
        + [dma((3, rows)), dma((3, rows)), dma((6,))]
        + [dma((rows, fold, CHUNKS)) for _ in range(3)]
        + [dma((cols, CHUNKS)), dma((CHUNKS,))]
        + job_scratch("fsdp"),
        compiler_params=pltpu.CompilerParams(
            collective_id=number, has_side_effects=True, vmem_limit_bytes=40 * 1024 * 1024
        ),
    )(*grads, *weights, codes)


def attend_kernel(
    group_size, query_ref, key_ref, value_ref, up_ref, cos_ref, sin_ref, norm_ref, allowed_ref,
    mixed_ref, query_grad_ref, key_grad_ref, value_grad_ref
):
    low = jnp.bfloat16
    factor = 1.0 / math.sqrt(DH)
    cosine, sine, norm = cos_ref[...], sin_ref[...], norm_ref[...]
    allowed = allowed_ref[...] > 0

    def total(ref, columns):
        parts = ref[0, :, columns].astype(jnp.float32)
        for r in range(1, ref.shape[0]):
            parts += ref[r, :, columns].astype(jnp.float32)
        return parts * norm

    def turned(values):
        return values * cosine + pltpu.roll(values, DH // 2, 1) * sine

    def turned_back(values):
        return values * cosine - pltpu.roll(values, DH // 2, 1) * sine

    key_rot = turned(total(key_ref, pl.ds(0, DH))).astype(low)
    value = total(value_ref, pl.ds(0, DH)).astype(low)
    key_grad = jnp.zeros(key_rot.shape, jnp.float32)
    value_grad = jnp.zeros(key_rot.shape, jnp.float32)
    for h in range(group_size):
        columns = pl.ds(h * DH, DH)
        query_rot = turned(total(query_ref, columns)).astype(low)
        scores = jnp.where(allowed, dot_last(query_rot, key_rot) * factor, NEG_FILL)
        exponent = jnp.exp(scores - jnp.max(scores, axis=-1, keepdims=True))
        probs = exponent / jnp.sum(exponent, axis=-1, keepdims=True)
        probs_low = probs.astype(low)
        upstream = up_ref[:, columns]
        mixed_ref[:, columns] = dot(probs_low, value).astype(low)
        prob_grad = dot_last(upstream, value)
        value_grad += dot_first(probs_low, upstream)
        score_grad = probs * (prob_grad - jnp.sum(probs * prob_grad, axis=-1, keepdims=True))
        score_low = score_grad.astype(low)
        query_grad_ref[:, columns] = turned_back(dot(score_low, key_rot) * factor).astype(low)
        key_grad += dot_first(score_low, query_rot) * factor
    key_grad_ref[...] = turned_back(key_grad).astype(low)
    value_grad_ref[...] = value_grad.astype(low)


def attend(query_parts, key_parts, value_parts, norm_factor, upstream, segment_row):
    rows, tokens, query_width = query_parts.shape
    pair_count = key_parts.shape[2] // DH
    wide = query_width // pair_count
    cosine, sine, allowed = rope_tables(segment_row, DH)
    fixed = pl.BlockSpec((tokens, DH), lambda g: (0, 0))
    parts = pl.BlockSpec((rows, tokens, DH), lambda g: (0, 0, g))
    one = pl.BlockSpec((tokens, DH), lambda g: (0, g))
    group = pl.BlockSpec((tokens, wide), lambda g: (0, g))
    low = jnp.bfloat16
    return pl.pallas_call(
        functools.partial(attend_kernel, wide // DH),
        grid=(pair_count,),
        out_shape=[
            jax.ShapeDtypeStruct((tokens, query_width), low),
            jax.ShapeDtypeStruct((tokens, query_width), low),
            jax.ShapeDtypeStruct((tokens, pair_count * DH), low),
            jax.ShapeDtypeStruct((tokens, pair_count * DH), low),
        ],
        in_specs=[
            pl.BlockSpec((rows, tokens, wide), lambda g: (0, 0, g)),
            parts, parts, group, fixed, fixed, fixed,
            pl.BlockSpec((tokens, tokens), lambda g: (0, 0)),
        ],
        out_specs=[group, group, one, one],
        compiler_params=pltpu.CompilerParams(vmem_limit_bytes=32 * 1024 * 1024),
    )(
        query_parts, key_parts, value_parts, upstream,
        jnp.concatenate([cosine, cosine], axis=1), jnp.concatenate([-sine, sine], axis=1),
        jnp.broadcast_to(norm_factor, (tokens, DH)), allowed.astype(jnp.float32),
    )


def code_back_kernel(chunk_ref, split_ref, out_ref, rows_out, send, recv, row_send, row_recv):
    sections, rows, cols = lax.axis_size("section"), lax.axis_size("fsdp"), lax.axis_size("tensor")
    s, f, t = lax.axis_index("section"), lax.axis_index("fsdp"), lax.axis_index("tensor")
    after, before = lax.rem(s + 1, sections), lax.rem(s + sections - 1, sections)
    barrier = pltpu.get_barrier_semaphore()
    for r in range(rows):
        for k in range(cols):
            pl.semaphore_signal(barrier, inc=1, device_id=(after, r, k), device_id_type=MESH)
    pl.semaphore_wait(barrier, rows * cols)
    copies, arrivals = [], []
    for k in range(cols):
        copies.append(
            sent(chunk_ref, out_ref.at[t], send.at[k], recv.at[t], (before, f, k))
        )
        arrivals.append(
            sent(chunk_ref, out_ref.at[k], send.at[k], recv.at[k], (before, f, k))
        )
        for r in range(rows):
            copies.append(
                sent(
                    split_ref.at[r], rows_out.at[f, t], row_send.at[r, k], row_recv.at[f, t],
                    (before, r, k),
                )
            )
            arrivals.append(
                sent(
                    split_ref.at[r], rows_out.at[r, k], row_send.at[r, k], row_recv.at[r, k],
                    (before, r, k),
                )
            )
    for copy in copies:
        copy.start()
    for copy in arrivals:
        copy.wait_recv()
    for copy in copies:
        copy.wait_send()


def code_back(number, chunk):
    rows, cols = lax.axis_size("fsdp"), lax.axis_size("tensor")
    dma = pltpu.SemaphoreType.DMA
    split = chunk.reshape(chunk.shape[0], rows, -1).transpose(1, 0, 2)
    return any_call(
        code_back_kernel,
        number,
        [
            jax.ShapeDtypeStruct((cols,) + chunk.shape, chunk.dtype),
            jax.ShapeDtypeStruct((rows, cols) + split.shape[1:], chunk.dtype),
        ],
        [dma((cols,)), dma((cols,)), dma((rows, cols)), dma((rows, cols))],
        chunk,
        split,
    )


def dot_last(left, right):
    return lax.dot_general(
        left, right, (((1,), (1,)), ((), ())), preferred_element_type=jnp.float32
    )


def dot_first(left, right):
    return lax.dot_general(
        left, right, (((0,), (0,)), ((), ())), preferred_element_type=jnp.float32
    )


def dot(left, right):
    return jnp.dot(left, right, preferred_element_type=jnp.float32)


def summed(parts):
    return jnp.sum(parts.astype(jnp.float32), axis=0)


def as_rows(row):
    return jnp.broadcast_to(row[None, :], (8, row.shape[0]))


def body(
    hidden,
    encoder_weight,
    decoder_weight,
    query_weight,
    key_weight,
    value_weight,
    segments,
    out_grad,
):
    low = jnp.bfloat16
    rows, cols = lax.axis_size("fsdp"), lax.axis_size("tensor")
    fold = cols // rows
    residual, encoder, decoder = hidden[0], encoder_weight[0], decoder_weight[0]
    wq, wk, wv = query_weight[0], key_weight[0], value_weight[0]
    tokens, width = residual.shape
    code_rows = encoder.shape[0]
    query_width, key_width = wq.shape[1], wk.shape[1]

    (hidden_all,) = exchange(0, (residual, "fsdp", "gather"))
    hidden_all = hidden_all.reshape(rows * tokens, width)
    chunk = rows * tokens // cols
    code_partial = dot_last(hidden_all, encoder).astype(low).reshape(cols, chunk, code_rows)
    split = code_rows // 2
    code_parts, decoder_upper = exchange(
        1, (code_partial, "tensor", "scatter"), (decoder[:split], "fsdp", "gather")
    )
    pieces, decoder_lower = code_forward(2, summed(code_parts).astype(low), decoder[split:])
    decoder_rows = jnp.concatenate([decoder_upper, decoder_lower], axis=1).reshape(-1, width)
    code_received = (
        pieces.reshape(rows, fold, chunk, code_rows)
        .transpose(1, 2, 0, 3)
        .reshape(tokens, rows * code_rows)
    )
    decoded = dot(code_received, decoder_rows)
    square_sum = jnp.sum(decoded * decoded, axis=1)
    columns, _, square_all = spread(3, decoded.astype(low), as_rows(square_sum))
    norm_factor = lax.rsqrt(jnp.sum(square_all[:, 0], axis=0) / D + NORM_EPS)[:, None]
    columns = columns.transpose(0, 2, 1, 3).reshape(rows * tokens, fold * width)
    query_parts, key_parts, value_parts = exchange(
        5,
        (dot(columns, wq).astype(low).reshape(rows, tokens, query_width), "fsdp", "scatter"),
        (dot(columns, wk).astype(low).reshape(rows, tokens, key_width), "fsdp", "scatter"),
        (dot(columns, wv).astype(low).reshape(rows, tokens, key_width), "fsdp", "scatter"),
    )
    query_parts, encoder = lax.optimization_barrier((query_parts, encoder))
    encoder_rows = lax.all_gather(encoder, "fsdp", axis=0, tiled=True)
    mixed, query_grad, key_grad, value_grad = attend(
        query_parts, key_parts, value_parts, norm_factor, out_grad[0], segments[0, 0]
    )
    code_split = code_received.reshape(tokens, rows, code_rows).transpose(1, 0, 2)
    grad_parts, code_all = back_to_features(
        6, (query_grad, key_grad, value_grad), (wq, wk, wv), code_split
    )
    whole = rows * tokens
    normed_grad = summed(grad_parts)
    (inner_parts,) = exchange(
        9, (as_rows(jnp.sum(normed_grad * decoded, axis=1)), "tensor", "gather")
    )
    inner_dot = jnp.sum(inner_parts[:, 0], axis=0)[:, None]
    decoded_grad = (norm_factor * normed_grad - decoded * norm_factor**3 * inner_dot / D).astype(
        low
    )
    grad_partial = dot_last(decoded_grad, decoder_rows).astype(low)
    code_grad_parts, decoded_grads = exchange(
        10,
        (grad_partial.reshape(cols, tokens // cols, rows * code_rows), "tensor", "scatter"),
        (decoded_grad, "fsdp", "gather"),
    )
    code_grad, code_grads = code_back(11, summed(code_grad_parts).astype(low))
    code_grad = code_grad.reshape(tokens, rows * code_rows)
    hidden_grad = dot(code_grad, encoder_rows).astype(low)
    decoder_grad = dot_first(
        code_all.reshape(whole, code_rows), decoded_grads.reshape(whole, width)
    )
    encoder_grad = dot_first(code_grads.reshape(whole, code_rows), hidden_all)
    return (mixed[None], hidden_grad[None], encoder_grad[None], decoder_grad[None])


def solution(mesh):
    placed = (
        P("section", "fsdp", "tensor"),
        P("section", "fsdp", "tensor"),
        P("section", "fsdp", "tensor"),
        P("section", "fsdp", "tensor"),
        P("section", "fsdp", "tensor"),
        P("section", "fsdp", "tensor"),
        P("section", "fsdp", None),
        P("section", "fsdp", "tensor"),
    )
    return jax.shard_map(
        body,
        mesh=mesh,
        in_specs=placed,
        out_specs=(
            P("section", "fsdp", "tensor"),
            P("section", "fsdp", "tensor"),
            P("section", "fsdp", "tensor"),
            P("section", "fsdp", "tensor"),
        ),
        check_vma=False,
    )
```

```python
import functools
import math

import jax
import jax.numpy as jnp
from jax import lax
from jax.experimental import pallas as pl
from jax.experimental.pallas import tpu as pltpu
from jax.sharding import PartitionSpec as P

D = 8192
DH = 128


NORM_EPS = 1e-05
ROPE_BASE = 500000.0
NEG_FILL = -1e30


def rope_tables(segment_row, dim):
    length = segment_row.shape[0]
    positions = jnp.arange(length, dtype=jnp.int32)
    earlier = jnp.sum((segment_row[None, :] < segment_row[:, None]).astype(jnp.int32), axis=1)
    places = (positions - earlier).astype(jnp.float32)
    frequency = jnp.exp(jnp.arange(0, dim, 2).astype(jnp.float32) * (-math.log(ROPE_BASE) / dim))
    angles = places[:, None] * frequency[None, :]
    allowed = (segment_row[None, :] == segment_row[:, None]) & (
        positions[None, :] <= positions[:, None]
    )
    return (jnp.cos(angles), jnp.sin(angles), allowed)


MESH = pl.DeviceIdType.MESH


CHUNKS = 4


def greet(axes):
    barrier = pltpu.get_barrier_semaphore()
    total = 0
    for axis in axes:
        size = lax.axis_size(axis)
        me = lax.axis_index(axis)
        for k in range(1, size):
            peer = lax.rem(me + k, size)
            pl.semaphore_signal(barrier, inc=1, device_id={axis: peer}, device_id_type=MESH)
        total += size - 1
    pl.semaphore_wait(barrier, total)


def sent(source, target, send, recv, place):
    return pltpu.make_async_remote_copy(
        src_ref=source,
        dst_ref=target,
        send_sem=send,
        recv_sem=recv,
        device_id=place,
        device_id_type=MESH,
    )


class Square:
    def __init__(self, axis, source, target, send, recv, own):
        self.axis, self.source, self.target = axis, source, target
        self.send, self.recv, self.own = send, recv, own
        self.me = lax.axis_index(axis)
        x, y = lax.rem(self.me, 2), self.me // 2
        self.near = (2 * y + (1 - x), 2 * (1 - y) + x)
        self.half = source.shape[0] // 2
        self.copies, self.arrivals = [], []

    def part(self, h):
        return pl.ds(h * self.half, self.half)

    def start(self):
        for order in range(2):
            for side in range(2):
                h = order if side == 0 else 1 - order
                copy = sent(
                    self.source.at[self.part(h)],
                    self.target.at[self.me, self.part(h)],
                    self.send.at[2 * side + h],
                    self.recv.at[2 * side + h],
                    {self.axis: self.near[side]},
                )
                copy.start()
                self.copies.append(copy)
        self.local = pltpu.make_async_copy(self.source, self.target.at[self.me], self.own)
        self.local.start()

    def arrival(self, slot, h, number):
        return sent(
            self.source.at[self.part(h)],
            self.target.at[slot, self.part(h)],
            self.send.at[number],
            self.recv.at[number],
            {self.axis: self.near[0]},
        )

    def forward(self):
        for side in range(2):
            h = side
            self.arrival(self.near[side], h, 2 * side + h).wait_recv()
            piece = self.target.at[self.near[side], self.part(h)]
            copy = sent(
                piece, piece, self.send.at[4 + h], self.recv.at[4 + h],
                {self.axis: self.near[1 - side]},
            )
            copy.start()
            self.copies.append(copy)

    def finish(self):
        for side in range(2):
            h = 1 - side
            self.arrival(self.near[side], h, 2 * side + h).wait_recv()
        for h in range(2):
            self.arrival(3 - self.me, h, 4 + h).wait_recv()
        for copy in self.copies:
            copy.wait_send()
        self.local.wait()


class Direct:
    def __init__(self, axis, mode, source, target, send, recv, own):
        self.axis, self.mode, self.source, self.target = axis, mode, source, target
        self.send, self.recv, self.own = send, recv, own
        self.copies = []

    def start(self):
        size, me = lax.axis_size(self.axis), lax.axis_index(self.axis)
        whole = self.mode == "gather"
        for k in range(1, size):
            peer = lax.rem(me + k, size)
            copy = sent(
                self.source if whole else self.source.at[peer],
                self.target.at[me],
                self.send.at[k],
                self.recv.at[k],
                {self.axis: peer},
            )
            copy.start()
            self.copies.append(copy)
        local = pltpu.make_async_copy(
            self.source if whole else self.source.at[me], self.target.at[me], self.own
        )
        local.start()
        self.copies.append(local)

    def forward(self):
        pass

    def finish(self):
        for copy in self.copies:
            copy.wait()


def transfer(axis, mode, *refs):
    if mode == "gather" and axis == "fsdp" and lax.axis_size(axis) == 4:
        return Square(axis, *refs)
    return Direct(axis, mode, *refs)


def exchange_kernel(jobs, *refs):
    count = len(jobs)
    ins, outs, sems = refs[:count], refs[count : 2 * count], refs[2 * count :]
    greet(sorted({axis for axis, _ in jobs}))
    moves = [
        transfer(axis, mode, ins[i], outs[i], *sems[3 * i : 3 * i + 3])
        for i, (axis, mode) in enumerate(jobs)
    ]
    for move in moves:
        move.start()
    for move in moves:
        move.forward()
    for move in moves:
        move.finish()


def job_scratch(axis):
    size = max(lax.axis_size(axis), 6)
    return [
        pltpu.SemaphoreType.DMA((size,)),
        pltpu.SemaphoreType.DMA((size,)),
        pltpu.SemaphoreType.DMA,
    ]


def any_call(kernel, number, shapes, scratch, *values):
    return pl.pallas_call(
        kernel,
        out_shape=shapes,
        in_specs=[pl.BlockSpec(memory_space=pl.ANY)] * len(values),
        out_specs=[pl.BlockSpec(memory_space=pl.ANY)] * len(shapes),
        scratch_shapes=scratch,
        compiler_params=pltpu.CompilerParams(collective_id=number, has_side_effects=True),
    )(*values)


def exchange(number, *work):
    jobs = tuple((axis, mode) for _, axis, mode in work)
    shapes, scratch = [], []
    for value, axis, mode in work:
        size = lax.axis_size(axis)
        shape = (size,) + value.shape if mode == "gather" else value.shape
        shapes.append(jax.ShapeDtypeStruct(shape, value.dtype))
        scratch += job_scratch(axis)
    return any_call(
        functools.partial(exchange_kernel, jobs), number, shapes, scratch,
        *[value for value, _, _ in work],
    )


def code_forward_kernel(chunk_ref, extra_ref, out_ref, extra_out, send, recv, *sems):
    sections, rows, cols = lax.axis_size("section"), lax.axis_size("fsdp"), lax.axis_size("tensor")
    s, f, t = lax.axis_index("section"), lax.axis_index("fsdp"), lax.axis_index("tensor")
    fold = cols // rows
    after, before = lax.rem(s + 1, sections), lax.rem(s + sections - 1, sections)
    barrier = pltpu.get_barrier_semaphore()
    for r in range(rows):
        for u in range(fold):
            pl.semaphore_signal(
                barrier, inc=1, device_id=(before, r, f * fold + u), device_id_type=MESH
            )
    for k in range(1, rows):
        pl.semaphore_signal(
            barrier, inc=1, device_id=(s, lax.rem(f + k, rows), t), device_id_type=MESH
        )
    pl.semaphore_wait(barrier, cols + rows - 1)
    slot = f * fold + lax.rem(t, fold)
    copies = []
    for k in range(cols):
        copy = sent(
            chunk_ref, out_ref.at[slot], send.at[k], recv.at[slot], (after, t // fold, k)
        )
        copy.start()
        copies.append(copy)
    move = transfer("fsdp", "gather", extra_ref, extra_out, *sems)
    move.start()
    move.forward()
    for k in range(cols):
        sent(
            chunk_ref, out_ref.at[k], send.at[k], recv.at[k], (after, t // fold, k)
        ).wait_recv()
    for copy in copies:
        copy.wait_send()
    move.finish()


def code_forward(number, chunk, extra):
    rows, cols = lax.axis_size("fsdp"), lax.axis_size("tensor")
    return any_call(
        code_forward_kernel,
        number,
        [
            jax.ShapeDtypeStruct((cols,) + chunk.shape, chunk.dtype),
            jax.ShapeDtypeStruct((rows,) + extra.shape, extra.dtype),
        ],
        [pltpu.SemaphoreType.DMA((cols,)), pltpu.SemaphoreType.DMA((cols,))]
        + job_scratch("fsdp"),
        chunk,
        extra,
    )


def spread_kernel(
    own_ref, sum_ref, columns_ref, gathered_ref, sums_ref,
    right_send, right_recv, left_send, left_recv, cross_send, cross_recv, own_sem, *sems
):
    rows, cols = lax.axis_size("fsdp"), lax.axis_size("tensor")
    f, t = lax.axis_index("fsdp"), lax.axis_index("tensor")
    fold = cols // rows
    size = own_ref.shape[0] // CHUNKS
    greet(("fsdp", "tensor"))
    sums = Direct("tensor", "gather", sum_ref, sums_ref, *sems)
    sums.start()

    def piece(ref, c):
        return ref.at[pl.ds(c * size, size)]

    def hop(d, c, block, way):
        source = piece(own_ref if d == 0 else gathered_ref.at[block], c)
        send, recv = (right_send, right_recv) if way > 0 else (left_send, left_recv)
        return sent(
            source, piece(gathered_ref.at[block], c), send.at[d, c], recv.at[d + 1, c],
            {"tensor": t + way},
        )

    def arrived(d, c, block, way):
        recv = right_recv if way > 0 else left_recv
        return sent(
            piece(own_ref, c), piece(gathered_ref.at[block], c), right_send.at[d, c],
            recv.at[d, c], {"tensor": lax.rem(t + 1, cols)},
        )

    def cross(source, c, block):
        target = piece(columns_ref.at[f, lax.rem(block, fold)], c)
        there = block // fold
        remote = sent(
            source, target, cross_send.at[block, c],
            cross_recv.at[f, lax.rem(block, fold), c], {"fsdp": there},
        )
        local = pltpu.make_async_copy(source, target, own_sem.at[lax.rem(block, fold), c])
        return there, remote, local

    def each(act):
        for d in range(cols):
            for c in range(CHUNKS):
                if d == 0:
                    act(d, c, t, 0)
                    continue

                @pl.when(t - d >= 0)
                def _():
                    act(d, c, t - d, 1)

                @pl.when(t + d < cols)
                def _():
                    act(d, c, t + d, -1)

    def begin(d, c, block, way):
        if d > 0:
            arrived(d, c, block, way).wait_recv()
        if way >= 0 and d < cols - 1:

            @pl.when(t + 1 < cols)
            def _():
                hop(d, c, block, 1).start()

        if way <= 0 and d < cols - 1:

            @pl.when(t > 0)
            def _():
                hop(d, c, block, -1).start()

        source = piece(own_ref if d == 0 else gathered_ref.at[block], c)
        there, remote, local = cross(source, c, block)

        @pl.when(there != f)
        def _():
            remote.start()

        @pl.when(there == f)
        def _():
            local.start()

    def end(d, c, block, way):
        if way >= 0 and d < cols - 1:

            @pl.when(t + 1 < cols)
            def _():
                hop(d, c, block, 1).wait_send()

        if way <= 0 and d < cols - 1:

            @pl.when(t > 0)
            def _():
                hop(d, c, block, -1).wait_send()

        source = piece(own_ref if d == 0 else gathered_ref.at[block], c)
        there, remote, local = cross(source, c, block)

        @pl.when(there != f)
        def _():
            remote.wait_send()

        @pl.when(there == f)
        def _():
            local.wait()

    each(begin)
    for k in range(1, rows):
        peer = lax.rem(f + k, rows)
        for u in range(fold):
            for c in range(CHUNKS):
                sent(
                    piece(own_ref, c), piece(columns_ref.at[peer, u], c), cross_send.at[0, c],
                    cross_recv.at[peer, u, c], {"fsdp": peer},
                ).wait_recv()
    each(end)
    sums.finish()


def spread(number, own, sums):
    rows, cols = lax.axis_size("fsdp"), lax.axis_size("tensor")
    fold = cols // rows
    dma = pltpu.SemaphoreType.DMA
    return any_call(
        spread_kernel,
        number,
        [
            jax.ShapeDtypeStruct((rows, fold) + own.shape, own.dtype),
            jax.ShapeDtypeStruct((cols,) + own.shape, own.dtype),
            jax.ShapeDtypeStruct((cols,) + sums.shape, sums.dtype),
        ],
        [dma((cols, CHUNKS)) for _ in range(5)]
        + [dma((rows, fold, CHUNKS)), dma((fold, CHUNKS))]
        + job_scratch("tensor"),
        own,
        sums,
    )


def back_kernel(
    *refs
):
    grads, weights, code_ref, (out_ref, code_out) = refs[:3], refs[3:6], refs[6], refs[7:9]
    held, loaded, (product_ref, middle_ref) = refs[9:12], refs[12:15], refs[15:17]
    gather_send, gather_recv, load_sem = refs[17:20]
    cross_send, cross_recv, send, recv, own_sem = refs[20:25]
    code_sems = refs[25:]
    rows, cols = lax.axis_size("fsdp"), lax.axis_size("tensor")
    f, t = lax.axis_index("fsdp"), lax.axis_index("tensor")
    fold = cols // rows
    width = product_ref.shape[3]
    size = product_ref.shape[2] // CHUNKS
    order = [0, 2, 1, 3] if rows == 4 else list(range(rows))
    loads = [
        pltpu.make_async_copy(weights[i], loaded[i], load_sem.at[i]) for i in range(3)
    ]
    owns = [
        pltpu.make_async_copy(grads[i], held[i].at[0], load_sem.at[3 + i]) for i in range(3)
    ]
    for copy in loads + owns:
        copy.start()
    greet(("fsdp", "tensor"))

    def away(k):
        return lax.rem(f + k, rows)

    def origin(k):
        return lax.rem(f + rows - k, rows)

    def spread_out(k, i):
        return sent(
            grads[i], held[i].at[k], gather_send.at[i, k], gather_recv.at[i, k],
            {"fsdp": away(k)},
        )

    for k in order[1:]:
        for i in range(3):
            spread_out(k, i).start()
    codes = Direct("fsdp", "scatter", code_ref, code_out, *code_sems)
    codes.start()

    def piece(ref, c):
        return ref.at[pl.ds(c * size, size)]

    def cross(k, u, c):
        return sent(
            piece(product_ref.at[k, u], c), piece(middle_ref.at[k, u], c),
            cross_send.at[k, u, c], cross_recv.at[k, u, c], {"fsdp": origin(k)},
        )

    def onward(k, u, c):
        block = away(k) * fold + u
        source = piece((product_ref if k == 0 else middle_ref).at[k, u], c)
        target = piece(out_ref.at[t], c)
        remote = sent(source, target, send.at[k, u, c], recv.at[t, c], {"tensor": block})
        return block, remote, pltpu.make_async_copy(source, target, own_sem.at[c])

    def pass_on(k, u, c):
        block, remote, local = onward(k, u, c)

        @pl.when(block != t)
        def _():
            remote.start()

        @pl.when(block == t)
        def _():
            local.start()

    for copy in loads + owns:
        copy.wait()
    tile = min(width, 512)
    for k in order:
        if k > 0:
            for i in range(3):
                spread_out(k, i).wait_recv()
        for u in range(fold):

            @pl.loop(0, width // tile)
            def _(n):
                lower = pl.multiple_of(u * width + n * tile, tile)
                total = dot_last(held[0][k], loaded[0][pl.ds(lower, tile), :])
                for i in range(1, 3):
                    total += dot_last(held[i][k], loaded[i][pl.ds(lower, tile), :])
                columns = pl.ds(pl.multiple_of(n * tile, tile), tile)
                product_ref[k, u, :, columns] = total.astype(product_ref.dtype)

            for c in range(CHUNKS):
                if k == 0:
                    pass_on(k, u, c)
                else:
                    cross(k, u, c).start()
    for k in order[1:]:
        for u in range(fold):
            for c in range(CHUNKS):
                cross(k, u, c).wait_recv()
                pass_on(k, u, c)
    for k in range(1, cols):
        peer = lax.rem(t + k, cols)
        for c in range(CHUNKS):
            sent(
                piece(middle_ref.at[0, 0], c), piece(out_ref.at[peer], c), send.at[0, 0, c],
                recv.at[peer, c], {"tensor": peer},
            ).wait_recv()
    for k in order:
        for i in range(3):
            if k > 0:
                spread_out(k, i).wait_send()
        for u in range(fold):
            for c in range(CHUNKS):
                if k > 0:
                    cross(k, u, c).wait_send()
                block, remote, local = onward(k, u, c)

                @pl.when(block != t)
                def _():
                    remote.wait_send()

                @pl.when(block == t)
                def _():
                    local.wait()

    codes.finish()


def back_to_features(number, grads, weights, codes):
    rows, cols = lax.axis_size("fsdp"), lax.axis_size("tensor")
    fold = cols // rows
    dma = pltpu.SemaphoreType.DMA
    tokens, low = grads[0].shape[0], jnp.bfloat16
    width = weights[0].shape[0] // fold
    return pl.pallas_call(
        back_kernel,
        out_shape=[
            jax.ShapeDtypeStruct((cols, tokens, width), low),
            jax.ShapeDtypeStruct(codes.shape, codes.dtype),
        ],
        in_specs=[pl.BlockSpec(memory_space=pl.ANY)] * 7,
        out_specs=[pl.BlockSpec(memory_space=pl.ANY)] * 2,
        scratch_shapes=[pltpu.VMEM((rows,) + grad.shape, low) for grad in grads]
        + [pltpu.VMEM(weight.shape, low) for weight in weights]
        + [pltpu.VMEM((rows, fold, tokens, width), low)] * 2
        + [dma((3, rows)), dma((3, rows)), dma((6,))]
        + [dma((rows, fold, CHUNKS)) for _ in range(3)]
        + [dma((cols, CHUNKS)), dma((CHUNKS,))]
        + job_scratch("fsdp"),
        compiler_params=pltpu.CompilerParams(
            collective_id=number, has_side_effects=True, vmem_limit_bytes=40 * 1024 * 1024
        ),
    )(*grads, *weights, codes)


def attend_kernel(
    group_size, query_ref, key_ref, value_ref, up_ref, cos_ref, sin_ref, norm_ref, allowed_ref,
    mixed_ref, query_grad_ref, key_grad_ref, value_grad_ref
):
    low = jnp.bfloat16
    factor = 1.0 / math.sqrt(DH)
    cosine, sine, norm = cos_ref[...], sin_ref[...], norm_ref[...]
    allowed = allowed_ref[...] > 0

    def total(ref, columns):
        parts = ref[0, :, columns].astype(jnp.float32)
        for r in range(1, ref.shape[0]):
            parts += ref[r, :, columns].astype(jnp.float32)
        return parts * norm

    def turned(values):
        return values * cosine + pltpu.roll(values, DH // 2, 1) * sine

    def turned_back(values):
        return values * cosine - pltpu.roll(values, DH // 2, 1) * sine

    key_rot = turned(total(key_ref, pl.ds(0, DH))).astype(low)
    value = total(value_ref, pl.ds(0, DH)).astype(low)
    key_grad = jnp.zeros(key_rot.shape, jnp.float32)
    value_grad = jnp.zeros(key_rot.shape, jnp.float32)
    for h in range(group_size):
        columns = pl.ds(h * DH, DH)
        query_rot = turned(total(query_ref, columns)).astype(low)
        scores = jnp.where(allowed, dot_last(query_rot, key_rot) * factor, NEG_FILL)
        exponent = jnp.exp(scores - jnp.max(scores, axis=-1, keepdims=True))
        probs = exponent / jnp.sum(exponent, axis=-1, keepdims=True)
        probs_low = probs.astype(low)
        upstream = up_ref[:, columns]
        mixed_ref[:, columns] = dot(probs_low, value).astype(low)
        prob_grad = dot_last(upstream, value)
        value_grad += dot_first(probs_low, upstream)
        score_grad = probs * (prob_grad - jnp.sum(probs * prob_grad, axis=-1, keepdims=True))
        score_low = score_grad.astype(low)
        query_grad_ref[:, columns] = turned_back(dot(score_low, key_rot) * factor).astype(low)
        key_grad += dot_first(score_low, query_rot) * factor
    key_grad_ref[...] = turned_back(key_grad).astype(low)
    value_grad_ref[...] = value_grad.astype(low)


def attend(query_parts, key_parts, value_parts, norm_factor, upstream, segment_row):
    rows, tokens, query_width = query_parts.shape
    pair_count = key_parts.shape[2] // DH
    wide = query_width // pair_count
    cosine, sine, allowed = rope_tables(segment_row, DH)
    fixed = pl.BlockSpec((tokens, DH), lambda g: (0, 0))
    parts = pl.BlockSpec((rows, tokens, DH), lambda g: (0, 0, g))
    one = pl.BlockSpec((tokens, DH), lambda g: (0, g))
    group = pl.BlockSpec((tokens, wide), lambda g: (0, g))
    low = jnp.bfloat16
    return pl.pallas_call(
        functools.partial(attend_kernel, wide // DH),
        grid=(pair_count,),
        out_shape=[
            jax.ShapeDtypeStruct((tokens, query_width), low),
            jax.ShapeDtypeStruct((tokens, query_width), low),
            jax.ShapeDtypeStruct((tokens, pair_count * DH), low),
            jax.ShapeDtypeStruct((tokens, pair_count * DH), low),
        ],
        in_specs=[
            pl.BlockSpec((rows, tokens, wide), lambda g: (0, 0, g)),
            parts, parts, group, fixed, fixed, fixed,
            pl.BlockSpec((tokens, tokens), lambda g: (0, 0)),
        ],
        out_specs=[group, group, one, one],
        compiler_params=pltpu.CompilerParams(vmem_limit_bytes=32 * 1024 * 1024),
    )(
        query_parts, key_parts, value_parts, upstream,
        jnp.concatenate([cosine, cosine], axis=1), jnp.concatenate([-sine, sine], axis=1),
        jnp.broadcast_to(norm_factor, (tokens, DH)), allowed.astype(jnp.float32),
    )


def code_back_kernel(chunk_ref, split_ref, out_ref, rows_out, send, recv, row_send, row_recv):
    sections, rows, cols = lax.axis_size("section"), lax.axis_size("fsdp"), lax.axis_size("tensor")
    s, f, t = lax.axis_index("section"), lax.axis_index("fsdp"), lax.axis_index("tensor")
    after, before = lax.rem(s + 1, sections), lax.rem(s + sections - 1, sections)
    barrier = pltpu.get_barrier_semaphore()
    for r in range(rows):
        for k in range(cols):
            pl.semaphore_signal(barrier, inc=1, device_id=(after, r, k), device_id_type=MESH)
    pl.semaphore_wait(barrier, rows * cols)
    copies, arrivals = [], []
    for k in range(cols):
        copies.append(
            sent(chunk_ref, out_ref.at[t], send.at[k], recv.at[t], (before, f, k))
        )
        arrivals.append(
            sent(chunk_ref, out_ref.at[k], send.at[k], recv.at[k], (before, f, k))
        )
        for r in range(rows):
            copies.append(
                sent(
                    split_ref.at[r], rows_out.at[f, t], row_send.at[r, k], row_recv.at[f, t],
                    (before, r, k),
                )
            )
            arrivals.append(
                sent(
                    split_ref.at[r], rows_out.at[r, k], row_send.at[r, k], row_recv.at[r, k],
                    (before, r, k),
                )
            )
    for copy in copies:
        copy.start()
    for copy in arrivals:
        copy.wait_recv()
    for copy in copies:
        copy.wait_send()


def code_back(number, chunk):
    rows, cols = lax.axis_size("fsdp"), lax.axis_size("tensor")
    dma = pltpu.SemaphoreType.DMA
    split = chunk.reshape(chunk.shape[0], rows, -1).transpose(1, 0, 2)
    return any_call(
        code_back_kernel,
        number,
        [
            jax.ShapeDtypeStruct((cols,) + chunk.shape, chunk.dtype),
            jax.ShapeDtypeStruct((rows, cols) + split.shape[1:], chunk.dtype),
        ],
        [dma((cols,)), dma((cols,)), dma((rows, cols)), dma((rows, cols))],
        chunk,
        split,
    )


def dot_last(left, right):
    return lax.dot_general(
        left, right, (((1,), (1,)), ((), ())), preferred_element_type=jnp.float32
    )


def dot_first(left, right):
    return lax.dot_general(
        left, right, (((0,), (0,)), ((), ())), preferred_element_type=jnp.float32
    )


def dot(left, right):
    return jnp.dot(left, right, preferred_element_type=jnp.float32)


def summed(parts):
    return jnp.sum(parts.astype(jnp.float32), axis=0)


def as_rows(row):
    return jnp.broadcast_to(row[None, :], (8, row.shape[0]))


def body(
    hidden,
    encoder_weight,
    decoder_weight,
    query_weight,
    key_weight,
    value_weight,
    segments,
    out_grad,
):
    low = jnp.bfloat16
    rows, cols = lax.axis_size("fsdp"), lax.axis_size("tensor")
    fold = cols // rows
    residual, encoder, decoder = hidden[0], encoder_weight[0], decoder_weight[0]
    wq, wk, wv = query_weight[0], key_weight[0], value_weight[0]
    tokens, width = residual.shape
    code_rows = encoder.shape[0]
    query_width, key_width = wq.shape[1], wk.shape[1]

    (hidden_all,) = exchange(0, (residual, "fsdp", "gather"))
    hidden_all = hidden_all.reshape(rows * tokens, width)
    chunk = rows * tokens // cols
    code_partial = dot_last(hidden_all, encoder).astype(low).reshape(cols, chunk, code_rows)
    split = code_rows // 2
    code_parts, decoder_upper = exchange(
        1, (code_partial, "tensor", "scatter"), (decoder[:split], "fsdp", "gather")
    )
    pieces, decoder_lower = code_forward(2, summed(code_parts).astype(low), decoder[split:])
    decoder_rows = jnp.concatenate([decoder_upper, decoder_lower], axis=1).reshape(-1, width)
    code_received = (
        pieces.reshape(rows, fold, chunk, code_rows)
        .transpose(1, 2, 0, 3)
        .reshape(tokens, rows * code_rows)
    )
    decoded = dot(code_received, decoder_rows)
    square_sum = jnp.sum(decoded * decoded, axis=1)
    columns, _, square_all = spread(3, decoded.astype(low), as_rows(square_sum))
    norm_factor = lax.rsqrt(jnp.sum(square_all[:, 0], axis=0) / D + NORM_EPS)[:, None]
    columns = columns.transpose(0, 2, 1, 3).reshape(rows * tokens, fold * width)
    query_parts, key_parts, value_parts = exchange(
        5,
        (dot(columns, wq).astype(low).reshape(rows, tokens, query_width), "fsdp", "scatter"),
        (dot(columns, wk).astype(low).reshape(rows, tokens, key_width), "fsdp", "scatter"),
        (dot(columns, wv).astype(low).reshape(rows, tokens, key_width), "fsdp", "scatter"),
    )
    mixed, query_grad, key_grad, value_grad = attend(
        query_parts, key_parts, value_parts, norm_factor, out_grad[0], segments[0, 0]
    )
    code_split = code_received.reshape(tokens, rows, code_rows).transpose(1, 0, 2)
    grad_parts, code_all = back_to_features(
        6, (query_grad, key_grad, value_grad), (wq, wk, wv), code_split
    )
    whole = rows * tokens
    normed_grad = summed(grad_parts)
    inner_parts, encoder_rows = exchange(
        9,
        (as_rows(jnp.sum(normed_grad * decoded, axis=1)), "tensor", "gather"),
        (encoder, "fsdp", "gather"),
    )
    encoder_rows = encoder_rows.reshape(rows * code_rows, width)
    inner_dot = jnp.sum(inner_parts[:, 0], axis=0)[:, None]
    decoded_grad = (norm_factor * normed_grad - decoded * norm_factor**3 * inner_dot / D).astype(
        low
    )
    grad_partial = dot_last(decoded_grad, decoder_rows).astype(low)
    code_grad_parts, decoded_grads = exchange(
        10,
        (grad_partial.reshape(cols, tokens // cols, rows * code_rows), "tensor", "scatter"),
        (decoded_grad, "fsdp", "gather"),
    )
    code_grad, code_grads = code_back(11, summed(code_grad_parts).astype(low))
    code_grad = code_grad.reshape(tokens, rows * code_rows)
    hidden_grad = dot(code_grad, encoder_rows).astype(low)
    decoder_grad = dot_first(
        code_all.reshape(whole, code_rows), decoded_grads.reshape(whole, width)
    )
    encoder_grad = dot_first(code_grads.reshape(whole, code_rows), hidden_all)
    return (mixed[None], hidden_grad[None], encoder_grad[None], decoder_grad[None])


def solution(mesh):
    placed = (
        P("section", "fsdp", "tensor"),
        P("section", "fsdp", "tensor"),
        P("section", "fsdp", "tensor"),
        P("section", "fsdp", "tensor"),
        P("section", "fsdp", "tensor"),
        P("section", "fsdp", "tensor"),
        P("section", "fsdp", None),
        P("section", "fsdp", "tensor"),
    )
    return jax.shard_map(
        body,
        mesh=mesh,
        in_specs=placed,
        out_specs=(
            P("section", "fsdp", "tensor"),
            P("section", "fsdp", "tensor"),
            P("section", "fsdp", "tensor"),
            P("section", "fsdp", "tensor"),
        ),
        check_vma=False,
    )
```
